512 devices in a mesh: group: 16 (over z), slab: 32 (over y, x, core).
Axes of the slice: x: 4, y: 4, z: 16, core: 2. Of those that a mesh axis runs over, the one named last changes fastest.
Arguments:
- operator: float32 [8192, 64, 448], P(('group', 'slab'))
- adjacency: int32 [8192, 6], P(('group', 'slab')), may hold values from -1 to 8191, as said below
- counts: int32 [8192], P(('group', 'slab')), may hold values from 1 to 6, as said below
- rhs: float32 [524288], P(('group', 'slab')), may hold values from -6 to 6
- start: float32 [524288], P(('group', 'slab')), may hold values from -6 to 6
- shifts: float32 [8], replicated, may hold values from 0.8 to 2.2
Outputs:
- solution: float32 [524288], P(('group', 'slab'))
- residual: float32 [524288], P(('group', 'slab'))
- upper: float32 [9, 9], replicated
The draws below stay inside these ranges and needn't reach their ends.
Inputs may be any that keep to these rules, and one draw needn't show every extreme that they name: Each element has 1 to 6 face neighbours; counts reach both ends in every draw. `adjacency`: entries f < counts[e] name an element other than e whose global number differs from e's by at most 2, so it lies on the same device or on the device just before or after it in the order group then slab; some element reaches a difference of 2 in every draw; entries f >= counts[e] are -1.
All inputs are finite; a program needn't handle non-finite values.
Results may differ from the reference program's by a relative error of at most 0.0008.
Values sent between devices are 32-bit elements; how exact they have to be, the bound alone decides.
No kernel may reach another device: no remote copies, remote signals or barrier semaphores. Data moves between devices by JAX's collectives and lax.ppermute only.
A program may use at most 64 MiB of HBM per device.

```python
import jax
import jax.numpy as jnp
from jax import lax

BS = 64
FACES = 6
S = 8
ELEM_DEV = 16
GHOST = 2
ELEMENTS = 8192


def layout_tables(key):
    total = ELEMENTS
    devices = ELEMENTS // ELEM_DEV
    key_count, key_step, key_sign, key_pick = jax.random.split(key, 4)
    glob = jnp.arange(total, dtype=jnp.int32)
    local = glob % ELEM_DEV
    owner = glob // ELEM_DEV
    counts = jax.random.randint(key_count, (total,), 1, FACES + 1).astype(jnp.int32)
    step = jax.random.randint(key_step, (total, FACES), 1, GHOST + 1).astype(jnp.int32)
    sign = 2 * jax.random.randint(key_sign, (total, FACES), 0, 2).astype(jnp.int32) - 1
    cand = glob[:, None] + sign * step
    cand = jnp.where((cand < 0) | (cand >= total), glob[:, None] - sign * step, cand)
    picked = jax.random.randint(key_pick, (devices,), 0, 2).astype(jnp.int32)
    picked = picked.at[0].set(1).at[1].set(1)
    chosen = picked[owner] == 1
    force_low = chosen & (owner >= 1) & (local < GHOST)
    force_high = chosen & (owner <= devices - 2) & (local >= ELEM_DEV - GHOST)
    faces = jnp.arange(FACES, dtype=jnp.int32)[None, :]
    cand = jnp.where(force_low[:, None] & (faces == 0), glob[:, None] - GHOST, cand)
    cand = jnp.where(force_high[:, None] & (faces == 1), glob[:, None] + GHOST, cand)
    counts = jnp.where(force_low | force_high, jnp.maximum(counts, 2), counts)
    counts = counts.at[0].set(FACES).at[1].set(1)
    valid = faces < counts[:, None]
    adjacency = jnp.where(valid, cand, -1).astype(jnp.int32)
    return (adjacency, counts)


def draw_adjacency(key, part):
    return layout_tables(key)[0]


def draw_counts(key, part):
    return layout_tables(key)[1]


def draw_operator(key, part):
    key = jax.random.fold_in(key, 11)
    shape = (ELEMENTS, BS, (FACES + 1) * BS)
    noise = jax.random.normal(key, shape, jnp.float32)
    noise = noise * (1.0 / jnp.sqrt(jnp.float32((FACES + 1) * BS)))
    rows = jnp.arange(BS)[:, None]
    cols = jnp.arange((FACES + 1) * BS)[None, :]
    diagonal = jnp.where(rows == cols, 1.5, 0.0).astype(jnp.float32)
    return (noise + diagonal[None, :, :]).astype(jnp.float32)


def steps_of(rng, shape, cuts, low, top_value):
    def one(position, shards_of):
        draws = jax.random.uniform(jax.random.fold_in(jax.random.fold_in(rng, 6), position), (shards_of,), jnp.float32, low / len(cuts), top_value / len(cuts))
        return jnp.repeat(jnp.exp(draws), shape[position] // shards_of).reshape((-1,) + (1,) * (len(shape) - position - 1))

    factor_of = one(*cuts[0])
    for cut in cuts[1:]:
        factor_of = factor_of * one(*cut)
    return factor_of


def scatter_about(own_key, extent, scale, bound, shards=(), held_as=jnp.bfloat16):
    values = jax.random.normal(own_key, extent, jnp.float32) * scale
    if len(shards) > 0:
        values = steps_of(own_key, extent, shards, -0.22, 0.18) * values
    return jnp.clip(values, min=-bound, max=bound).astype(held_as)


def setup_inputs(seed: int = 0) -> dict:
    key_of = jax.random.split(jax.random.key(seed), 7)
    operator = draw_operator(jax.random.fold_in(key_of[6], 71), 0)
    adjacency = draw_adjacency(jax.random.fold_in(key_of[6], 71), 0)
    counts = draw_counts(jax.random.fold_in(key_of[6], 71), 0)
    rhs = scatter_about(key_of[3], (ELEMENTS * BS,), 1.0, 6.0, ((0, 512),), jnp.float32)
    start = scatter_about(key_of[4], (ELEMENTS * BS,), 1.0, 6.0, ((0, 512),), jnp.float32)
    shifts = jnp.clip(jax.random.uniform(key_of[5], (S,), jnp.float32, 0.8, 2.2), 0.8, 2.2)
    return {"operator": operator, "adjacency": adjacency, "counts": counts, "rhs": rhs, "start": start, "shifts": shifts}


def apply_operator(operator, adjacency, counts, vec):
    valid = jnp.arange(FACES)[None, :] < counts[:, None]
    near = vec[jnp.maximum(adjacency, 0)]
    near = jnp.where(valid[:, :, None], near, 0.0)
    stacked = jnp.concatenate([vec[:, None, :], near], axis=1).reshape(vec.shape[0], (FACES + 1) * BS)
    return jnp.einsum('eij,ej->ei', operator, stacked, precision=lax.Precision.HIGHEST)

def positive_qr(matrix):
    factor = jnp.linalg.qr(matrix, mode='r')
    factor = factor[:matrix.shape[1], :]
    signs = jnp.where(jnp.diagonal(factor) >= 0, 1.0, -1.0)
    return factor * signs[:, None]

def back_solve(triangle, target):
    length = target.shape[0]
    result = jnp.zeros_like(target)
    for index in range(length - 1, -1, -1):
        partial_sum = jnp.sum(triangle[index] * result)
        result = result.at[index].set((target[index] - partial_sum) / triangle[index, index])
    return result

def reference(operator, adjacency, counts, rhs, start, shifts):
    x_start = start.reshape(ELEMENTS, BS)
    first = rhs.reshape(ELEMENTS, BS) - apply_operator(operator, adjacency, counts, x_start)
    vectors = [first]
    for step in range(S):
        vectors.append(apply_operator(operator, adjacency, counts, vectors[-1]) - shifts[step] * vectors[-1])
    basis = jnp.stack(vectors).reshape(S + 1, ELEMENTS * BS)
    factor = positive_qr(basis.T)
    bidiag = jnp.eye(S + 1, S, dtype=jnp.float32) * shifts[None, :] + jnp.eye(S + 1, S, k=-1, dtype=jnp.float32)
    hess = jnp.dot(factor, bidiag, precision=lax.Precision.HIGHEST)
    augmented = jnp.concatenate([hess, factor[:, 0:1]], axis=1)
    second = positive_qr(augmented)
    coeffs = back_solve(second[:S, :S], second[:S, S])
    solution = start + jnp.dot(coeffs, basis[:S], precision=lax.Precision.HIGHEST)
    moved = basis[1:] + shifts[:, None] * basis[:S]
    residual = first.reshape(-1) - jnp.dot(coeffs, moved, precision=lax.Precision.HIGHEST)
    upper = factor / jnp.sqrt(jnp.float32(ELEMENTS * BS))
    return (solution, residual, upper)
```

```python
import functools

import jax
import jax.numpy as jnp
from jax import lax
from jax.experimental import pallas as pl
from jax.experimental.pallas import tpu as pltpu
from jax.sharding import PartitionSpec as P

AXES = ("group", "slab")
WIDTH = 64
LANES = 128
REACH = 2
BANDS = 2 * REACH + 1
HALF = WIDTH // 2
ROWS = BANDS * HALF
PAD = 8


def shifted(array, by):
    size = lax.axis_size(AXES)
    pairs = [(i, i + by) for i in range(size) if 0 <= i + by < size]
    return lax.ppermute(array, AXES, pairs)


def lane_ids(rows):
    return lax.broadcasted_iota(jnp.int32, (rows, LANES), 1)


def band_kernel(op_ref, adj_ref, counts_ref, start_ref, rhs_ref, out_ref):
    elems, _, columns = op_ref.shape
    faces = columns // WIDTH - 1
    base = lax.axis_index(AXES) * elems
    left = lane_ids(HALF) < WIDTH

    def one(e, carry):
        blocks = []
        for tile in range(columns // LANES):
            lanes = pl.ds(tile * LANES, LANES)
            top = op_ref[e, pl.ds(0, HALF), lanes]
            low = op_ref[e, pl.ds(HALF, HALF), lanes]
            blocks.append(jnp.where(left, top, pltpu.roll(low, WIDTH, 1)))
            blocks.append(jnp.where(left, pltpu.roll(top, WIDTH, 1), low))
        if columns % LANES:
            lanes = pl.ds(columns - WIDTH, WIDTH)
            top = op_ref[e, pl.ds(0, HALF), lanes]
            low = op_ref[e, pl.ds(HALF, HALF), lanes]
            blocks.append(jnp.concatenate([top, low], axis=1))
        count = counts_ref[e]
        place = []
        for face in range(faces):
            offset = adj_ref[face, e] - (base + e) + REACH
            place.append(jnp.where(face < count, offset, -1))
        for band in range(BANDS):
            rows = pl.ds(pl.multiple_of(e * ROWS + band * HALF, HALF), HALF)
            total = blocks[0] if band == REACH else None
            if band != REACH:
                for face in range(faces):
                    weight = jnp.where(place[face] == band, jnp.float32(1), jnp.float32(0))
                    term = blocks[face + 1] * weight
                    total = term if total is None else total + term
            out_ref[rows, :] = total
        return carry

    lax.fori_loop(0, elems, one, 0)
    tail = elems * ROWS
    out_ref[pl.ds(tail, 8), :] = start_ref[...]
    out_ref[pl.ds(tail + 8, 8), :] = rhs_ref[...]


def basis_kernel(
    elems, steps, copies,
    below_ref, own_ref, above_ref, far_low_ref, far_high_ref, shifts_ref,
    basis_ref, gram_ref,
    held, vecs, given, sems,
):
    block = elems * ROWS + 16
    sources = (below_ref, own_ref, above_ref)
    moves = [
        pltpu.make_async_copy(source, held.at[pl.ds(part * block, block), :], sems.at[part])
        for part, source in enumerate(sources)
    ]
    for move in moves:
        move.start()
    level = vecs.shape[0] // (steps + 2)
    lane = lane_ids(8)
    left8 = lane < WIDTH
    lane_h = lane_ids(HALF)
    row_h = lax.broadcasted_iota(jnp.int32, (HALF, LANES), 0)
    left = lane_h < WIDTH
    spot = lane_h % WIDTH
    pick_top = spot == row_h
    pick_low = spot == row_h + HALF
    for move in moves:
        move.wait()

    def spread(ref, row, packed):
        turned = pltpu.roll(packed, WIDTH, 1)
        ref[pl.ds(row, 8, stride=2), :] = jnp.where(left8, packed, turned)
        ref[pl.ds(row + 1, 8, stride=2), :] = jnp.where(left8, turned, packed)

    for part in range(3):
        tail = part * block + elems * ROWS
        spread(vecs, PAD + part * elems, held[pl.ds(tail, 8), :])
        spread(given, part * elems, held[pl.ds(tail + 8, 8), :])
    for ref, row in ((far_low_ref, PAD - 2), (far_high_ref, PAD + 3 * elems)):
        packed = jnp.broadcast_to(ref[...], (8, LANES))
        turned = pltpu.roll(packed, WIDTH, 1)
        vecs[pl.ds(row, 1), :] = jnp.where(left8, packed, turned)[:1]
        vecs[pl.ds(row + 1, 1), :] = jnp.where(left8, turned, packed)[:1]

    def times(e, at):
        first = e * ROWS + (e // elems) * 16
        total = None
        for band in range(BANDS):
            rows = pl.ds(pl.multiple_of(first + band * HALF, 16), HALF)
            near = vecs[pl.ds(at + e + (band - REACH), 1), :]
            term = held[rows, :] * near
            total = term if total is None else total + term
        top = jnp.sum(jnp.where(left, total, 0.0), axis=1, keepdims=True)
        low = jnp.sum(jnp.where(left, 0.0, total), axis=1, keepdims=True)
        placed = jnp.where(pick_top, top, jnp.where(pick_low, low, 0.0))
        return jnp.sum(placed, axis=0, keepdims=True)

    unroll = 4

    def residual_group(group, carry):
        for k in range(unroll):
            e = group * unroll + k
            vecs[pl.ds(level + PAD + e, 1), :] = given[pl.ds(e, 1), :] - times(e, PAD)
        return carry

    lax.fori_loop(0, 3 * elems // unroll, residual_group, 0)

    def step(index, carry):
        at = (index + 1) * level + PAD
        shift = shifts_ref[index]
        first = REACH * (index + 1)

        def group(number, inner):
            for k in range(unroll):
                e = first + number * unroll + k
                vecs[pl.ds(at + level + e, 1), :] = times(e, at) - shift * vecs[pl.ds(at + e, 1), :]
            return inner

        lax.fori_loop(0, (3 * elems - 2 * first) // unroll, group, 0)
        return carry

    lax.fori_loop(0, steps, step, 0)

    rows = []
    for k in range(steps + 1):
        at = (k + 1) * level + PAD + elems
        packed = jnp.where(left8, vecs[pl.ds(at, 8, stride=2), :], vecs[pl.ds(at + 1, 8, stride=2), :])
        basis_ref[pl.ds(8 * k, 8), :] = packed
        rows.append(packed)
    total = jnp.zeros((8, LANES), jnp.float32)
    number = 0
    for i in range(steps + 1):
        for j in range(i, steps + 1):
            entry = jnp.sum(rows[i] * rows[j], axis=1, keepdims=True)
            total = jnp.where(lane == number, entry, total)
            number += 1
    gram = jnp.sum(total, axis=0, keepdims=True)
    gram_ref[...] = jnp.broadcast_to(gram, (copies, LANES))


def partial_kernel(copies, parts_ref, out_ref):
    total = jnp.sum(parts_ref[...], axis=0, keepdims=True)
    out_ref[...] = jnp.broadcast_to(total, (copies, LANES))


def inverse_root(value):
    guess = lax.rsqrt(value)
    return guess * (1.5 - 0.5 * value * guess * guess)


def finish_kernel(count, steps, parts_ref, basis_ref, start_ref, shifts_ref, sol_ref, res_ref, upper_ref):
    size = steps + 1
    lane = lane_ids(8)
    summed = jnp.broadcast_to(jnp.sum(parts_ref[...], axis=0, keepdims=True), (8, LANES))
    gram = {}
    number = 0
    for i in range(size):
        for j in range(i, size):
            entry = jnp.sum(jnp.where(lane == number, summed, 0.0), axis=1, keepdims=True)
            gram[i, j] = jnp.broadcast_to(entry, (8, LANES))
            number += 1
    factor = {}
    for k in range(size):
        turn = inverse_root(gram[k, k])
        for j in range(k, size):
            factor[k, j] = gram[k, j] * turn
        for i in range(k + 1, size):
            for j in range(i, size):
                gram[i, j] = gram[i, j] - factor[k, i] * factor[k, j]
    hess = {}
    for k in range(steps):
        for i in range(k + 1):
            hess[i, k] = factor[i, k] * shifts_ref[k] + factor[i, k + 1]
        hess[k + 1, k] = factor[k + 1, k + 1]
    target = [factor[0, 0]] + [jnp.zeros((8, LANES), jnp.float32)] * steps
    inverse = []
    for k in range(steps):
        a, b = hess[k, k], hess[k + 1, k]
        scale = inverse_root(a * a + b * b)
        cos, sin = a * scale, b * scale
        inverse.append(scale)
        for j in range(k + 1, steps):
            up, down = hess[k, j], hess[k + 1, j]
            hess[k, j] = cos * up + sin * down
            hess[k + 1, j] = cos * down - sin * up
        target[k], target[k + 1] = cos * target[k], -(sin * target[k])
    coeffs = [None] * steps
    for k in range(steps - 1, -1, -1):
        value = target[k]
        for j in range(k + 1, steps):
            value = value - hess[k, j] * coeffs[j]
        coeffs[k] = value * inverse[k]
    rows = [basis_ref[pl.ds(8 * k, 8), :] for k in range(size)]
    sol, res = 0.0, 0.0
    for k in range(steps):
        sol = sol + coeffs[k] * rows[k]
        res = res + coeffs[k] * (rows[k + 1] + shifts_ref[k] * rows[k])
    sol_ref[...] = start_ref[...] + sol
    res_ref[...] = rows[0] - res
    wide = lane_ids(16)
    tall = lax.broadcasted_iota(jnp.int32, (16, LANES), 0)
    scale = 1.0 / (count ** 0.5)
    upper = jnp.zeros((16, LANES), jnp.float32)
    for i in range(size):
        for j in range(i, size):
            entry = jnp.concatenate([factor[i, j]] * 2, axis=0) * scale
            upper = jnp.where((wide == j) & (tall == i), entry, upper)
    upper_ref[...] = upper[:size, :size]


def body(operator, adjacency, counts, rhs, start, shifts):
    elems, width, columns = operator.shape
    steps = shifts.shape[0]
    devices = lax.axis_size(AXES)
    slabs = lax.axis_size("slab")
    groups = lax.axis_size("group")
    packed = elems * width // LANES
    block = elems * ROWS + 2 * packed
    vmem = pl.BlockSpec(memory_space=pltpu.VMEM)
    smem = pl.BlockSpec(memory_space=pltpu.SMEM)
    hbm = pl.BlockSpec(memory_space=pl.ANY)
    params = pltpu.CompilerParams(vmem_limit_bytes=32 * 1024 * 1024)
    f32 = jnp.float32

    x = start.reshape(packed, LANES)
    b = rhs.reshape(packed, LANES)
    far_low = shifted(x[packed - 1 :], 2)
    far_high = shifted(x[:1], -2)
    own = pl.pallas_call(
        band_kernel,
        out_shape=jax.ShapeDtypeStruct((block, LANES), f32),
        in_specs=[vmem, smem, smem, vmem, vmem],
        out_specs=vmem,
        compiler_params=params,
        name="bands",
    )(operator, adjacency.T, counts, x, b)
    below = shifted(own, 1)
    above = shifted(own, -1)
    basis, gram = pl.pallas_call(
        functools.partial(basis_kernel, elems, steps, slabs),
        out_shape=(
            jax.ShapeDtypeStruct((8 * (steps + 1), LANES), f32),
            jax.ShapeDtypeStruct((slabs, LANES), f32),
        ),
        in_specs=[hbm, hbm, hbm, vmem, vmem, smem],
        out_specs=(vmem, vmem),
        scratch_shapes=[
            pltpu.VMEM((3 * block, LANES), f32),
            pltpu.VMEM(((steps + 2) * (3 * elems + 2 * PAD), LANES), f32),
            pltpu.VMEM((3 * elems, LANES), f32),
            pltpu.SemaphoreType.DMA((3,)),
        ],
        compiler_params=params,
        name="basis",
    )(below, own, above, far_low, far_high, shifts)
    by_slab = lax.all_to_all(gram, "slab", 0, 0, tiled=True)
    partial = pl.pallas_call(
        functools.partial(partial_kernel, groups),
        out_shape=jax.ShapeDtypeStruct((groups, LANES), f32),
        in_specs=[vmem],
        out_specs=vmem,
        name="partial",
    )(by_slab)
    by_group = lax.all_to_all(partial, "group", 0, 0, tiled=True)
    sol, res, upper = pl.pallas_call(
        functools.partial(finish_kernel, devices * elems * width, steps),
        out_shape=(
            jax.ShapeDtypeStruct((packed, LANES), f32),
            jax.ShapeDtypeStruct((packed, LANES), f32),
            jax.ShapeDtypeStruct((steps + 1, steps + 1), f32),
        ),
        in_specs=[vmem, vmem, vmem, smem],
        out_specs=(vmem, vmem, vmem),
        name="finish",
    )(by_group, basis, x, shifts)
    return (sol.reshape(-1), res.reshape(-1), upper)


def solution(mesh):
    split = P(AXES)
    return jax.shard_map(
        body,
        mesh=mesh,
        in_specs=(P(AXES, None, None), P(AXES, None), split, split, split, P()),
        out_specs=(split, split, P()),
        check_vma=False,
    )
```

```python
import functools

import jax
import jax.numpy as jnp
from jax import lax
from jax.experimental import pallas as pl
from jax.experimental.pallas import tpu as pltpu
from jax.sharding import PartitionSpec as P

AXES = ("group", "slab")
WIDTH = 64
LANES = 128
REACH = 2
BANDS = 2 * REACH + 1
HALF = WIDTH // 2
ROWS = BANDS * HALF
CHUNK = 4
PAD = 8


def shifted(array, by):
    size = lax.axis_size(AXES)
    pairs = [(i, i + by) for i in range(size) if 0 <= i + by < size]
    return lax.ppermute(array, AXES, pairs)


def lane_ids(rows):
    return lax.broadcasted_iota(jnp.int32, (rows, LANES), 1)


def band_kernel(op_ref, adj_ref, counts_ref, start_ref, rhs_ref, out_ref, held, made, in_sems, out_sems):
    elems, _, columns = op_ref.shape
    faces = columns // WIDTH - 1
    chunks = elems // CHUNK
    base = lax.axis_index(AXES) * elems
    left = lane_ids(HALF) < WIDTH
    tail = elems * ROWS

    def arriving(chunk):
        part = pl.ds(chunk * CHUNK, CHUNK)
        return pltpu.make_async_copy(op_ref.at[part], held.at[part], in_sems.at[chunk])

    def leaving(chunk):
        size = CHUNK * ROWS
        part = pl.ds(pl.multiple_of(chunk * size, size), size)
        return pltpu.make_async_copy(made.at[part, :], out_ref.at[part, :], out_sems.at[chunk])

    for chunk in range(chunks):
        arriving(chunk).start()
    extras = [
        pltpu.make_async_copy(start_ref, out_ref.at[pl.ds(tail, 8), :], out_sems.at[chunks]),
        pltpu.make_async_copy(rhs_ref, out_ref.at[pl.ds(tail + 8, 8), :], out_sems.at[chunks + 1]),
    ]
    for extra in extras:
        extra.start()

    def one(e):
        blocks = []
        for tile in range(columns // LANES):
            lanes = pl.ds(tile * LANES, LANES)
            top = held[e, pl.ds(0, HALF), lanes]
            low = held[e, pl.ds(HALF, HALF), lanes]
            blocks.append(jnp.where(left, top, pltpu.roll(low, WIDTH, 1)))
            blocks.append(jnp.where(left, pltpu.roll(top, WIDTH, 1), low))
        if columns % LANES:
            lanes = pl.ds(columns - WIDTH, WIDTH)
            top = held[e, pl.ds(0, HALF), lanes]
            low = held[e, pl.ds(HALF, HALF), lanes]
            blocks.append(jnp.concatenate([top, low], axis=1))
        count = counts_ref[e]
        place = []
        for face in range(faces):
            offset = adj_ref[face, e] - (base + e) + REACH
            place.append(jnp.where(face < count, offset, -1))
        for band in range(BANDS):
            rows = pl.ds(pl.multiple_of(e * ROWS + band * HALF, HALF), HALF)
            total = blocks[0] if band == REACH else None
            if band != REACH:
                for face in range(faces):
                    weight = jnp.where(place[face] == band, jnp.float32(1), jnp.float32(0))
                    term = blocks[face + 1] * weight
                    total = term if total is None else total + term
            made[rows, :] = total

    def some(chunk, carry):
        arriving(chunk).wait()
        for k in range(CHUNK):
            one(chunk * CHUNK + k)
        leaving(chunk).start()
        return carry

    lax.fori_loop(0, chunks, some, 0)
    for chunk in range(chunks):
        leaving(chunk).wait()
    for extra in extras:
        extra.wait()


def stacked_sums(terms, row):
    for span in (4, 2, 1):
        low = (row & span) == 0
        half = len(terms) // 2
        merged = []
        for a, b in zip(terms[:half], terms[half:]):
            kept = jnp.where(low, a, b)
            if span == 4:
                moved = pltpu.roll(jnp.where(low, b, a), 4, 0)
            else:
                moved = jnp.where(low, pltpu.roll(a, 8 - span, 0), pltpu.roll(b, span, 0))
            merged.append(kept + moved)
        terms = merged
    return terms[0]


def basis_kernel(
    elems, steps,
    below_ref, own_ref, above_ref, far_low_ref, far_high_ref, shifts_ref,
    basis_ref, gram_ref,
    vecs,
):
    refs = (below_ref, own_ref, above_ref)
    level = 3 * elems + 2 * PAD
    given = (steps + 2) * level
    lane = lane_ids(8)
    row = lax.broadcasted_iota(jnp.int32, (8, LANES), 0)
    left = lane < WIDTH
    half = lane_ids(HALF)
    left_half = half < WIDTH
    pick_top = half % WIDTH == lax.broadcasted_iota(jnp.int32, (HALF, LANES), 0)
    pick_low = half % WIDTH == lax.broadcasted_iota(jnp.int32, (HALF, LANES), 0) + HALF

    empty = jnp.zeros((8, LANES), jnp.float32)
    for at in range(0, vecs.shape[0], 8):
        vecs[pl.ds(at, 8), :] = empty

    def spread(at, packed):
        turned = pltpu.roll(packed, WIDTH, 1)
        vecs[pl.ds(at, 8, stride=2), :] = jnp.where(left, packed, turned)
        vecs[pl.ds(at + 1, 8, stride=2), :] = jnp.where(left, turned, packed)

    for part, ref in enumerate(refs):
        tail = elems * ROWS
        spread(PAD + part * elems, ref[pl.ds(tail, 8), :])
        spread(given + PAD + part * elems, ref[pl.ds(tail + 8, 8), :])
    for ref, at in ((far_low_ref, PAD - 2), (far_high_ref, PAD + 3 * elems)):
        packed = jnp.broadcast_to(ref[...], (8, LANES))
        turned = pltpu.roll(packed, WIDTH, 1)
        vecs[pl.ds(at, 1), :] = jnp.where(left, packed, turned)[:1]
        vecs[pl.ds(at + 1, 1), :] = jnp.where(left, turned, packed)[:1]

    def times(part, first, at):
        near = [vecs[pl.ds(at + (k - REACH), 1), :] for k in range(8 + 2 * REACH)]
        terms = []
        for k in range(8):
            total = None
            for band in range(BANDS):
                rows = pl.ds((first + k) * ROWS + band * HALF, HALF)
                term = refs[part][rows, :] * near[k + band]
                total = term if total is None else total + term
            top = jnp.sum(jnp.where(left_half, total, 0.0), axis=1, keepdims=True)
            low = jnp.sum(jnp.where(left_half, 0.0, total), axis=1, keepdims=True)
            placed = jnp.where(pick_top, top, jnp.where(pick_low, low, 0.0))
            terms.append(jnp.sum(placed.reshape(HALF // 8, 8, LANES), axis=0))
        return stacked_sums(terms, row)

    def apply(index, groups):
        at = pl.multiple_of(index * level + PAD, 8)
        if isinstance(index, int):
            opening = index == 0
            source = given + PAD if opening else at
            sign, scale = (-1.0, 1.0) if opening else (1.0, -shifts_ref[index - 1])
        else:
            opening = index == 0
            source = pl.multiple_of(jnp.where(opening, given + PAD, at), 8)
            sign = jnp.where(opening, jnp.float32(-1), jnp.float32(1))
            scale = jnp.where(opening, jnp.float32(1), -shifts_ref[jnp.maximum(index - 1, 0)])
        made = []
        for part, first in groups:
            place = part * elems + first
            fresh = times(part, first, at + place)
            made.append((place, sign * fresh + scale * vecs[pl.ds(source + place, 8), :]))
        for place, value in made:
            vecs[pl.ds(at + level + place, 8), :] = value

    own = [(1, first) for first in range(0, elems, 8)]
    groups = [(part, first) for part in (0, 2) for first in range(0, elems, 8)]
    done = 0
    while done <= steps:
        reach = REACH * (steps - done)
        wanted = [
            (part, first)
            for part, first in groups
            if (elems - first - 8 < reach if part == 0 else first < reach)
        ]
        until = done
        while until <= steps:
            later = REACH * (steps - until)
            if wanted != [
                (part, first)
                for part, first in groups
                if (elems - first - 8 < later if part == 0 else first < later)
            ]:
                break
            until += 1

        def turn(index, carry, wanted=wanted):
            apply(index, wanted + own)
            return carry

        if until - done == 1:
            apply(done, wanted + own)
        else:
            lax.fori_loop(done, until, turn, 0)
        done = until

    rows = []
    for k in range(steps + 1):
        at = (k + 1) * level + PAD + elems
        packed = jnp.where(left, vecs[pl.ds(at, 8, stride=2), :], vecs[pl.ds(at + 1, 8, stride=2), :])
        basis_ref[pl.ds(8 * k, 8), :] = packed
        rows.append(packed)
    total = jnp.zeros((8, LANES), jnp.float32)
    number = 0
    for i in range(steps + 1):
        for j in range(i, steps + 1):
            entry = jnp.sum(rows[i] * rows[j], axis=1, keepdims=True)
            total = jnp.where(lane == number, entry, total)
            number += 1
    gram_ref[...] = jnp.sum(total, axis=0, keepdims=True)


def inverse_root(value):
    guess = lax.rsqrt(value)
    return guess * (1.5 - 0.5 * value * guess * guess)


def finish_kernel(count, steps, parts_ref, basis_ref, start_ref, shifts_ref, sol_ref, res_ref, upper_ref):
    size = steps + 1
    lane = lane_ids(8)
    summed = jnp.broadcast_to(jnp.sum(parts_ref[...], axis=0, keepdims=True), (8, LANES))
    gram = {}
    number = 0
    for i in range(size):
        for j in range(i, size):
            entry = jnp.sum(jnp.where(lane == number, summed, 0.0), axis=1, keepdims=True)
            gram[i, j] = jnp.broadcast_to(entry, (8, LANES))
            number += 1
    factor = {}
    for k in range(size):
        turn = inverse_root(gram[k, k])
        for j in range(k, size):
            factor[k, j] = gram[k, j] * turn
        for i in range(k + 1, size):
            for j in range(i, size):
                gram[i, j] = gram[i, j] - factor[k, i] * factor[k, j]
    hess = {}
    for k in range(steps):
        for i in range(k + 1):
            hess[i, k] = factor[i, k] * shifts_ref[k] + factor[i, k + 1]
        hess[k + 1, k] = factor[k + 1, k + 1]
    target = [factor[0, 0]] + [jnp.zeros((8, LANES), jnp.float32)] * steps
    inverse = []
    for k in range(steps):
        a, b = hess[k, k], hess[k + 1, k]
        scale = inverse_root(a * a + b * b)
        cos, sin = a * scale, b * scale
        inverse.append(scale)
        for j in range(k + 1, steps):
            up, down = hess[k, j], hess[k + 1, j]
            hess[k, j] = cos * up + sin * down
            hess[k + 1, j] = cos * down - sin * up
        target[k], target[k + 1] = cos * target[k], -(sin * target[k])
    coeffs = [None] * steps
    for k in range(steps - 1, -1, -1):
        value = target[k]
        for j in range(k + 1, steps):
            value = value - hess[k, j] * coeffs[j]
        coeffs[k] = value * inverse[k]
    rows = [basis_ref[pl.ds(8 * k, 8), :] for k in range(size)]
    sol, res = 0.0, 0.0
    for k in range(steps):
        sol = sol + coeffs[k] * rows[k]
        res = res + coeffs[k] * (rows[k + 1] + shifts_ref[k] * rows[k])
    sol_ref[...] = start_ref[...] + sol
    res_ref[...] = rows[0] - res
    wide = lane_ids(16)
    tall = lax.broadcasted_iota(jnp.int32, (16, LANES), 0)
    scale = 1.0 / (count ** 0.5)
    upper = jnp.zeros((16, LANES), jnp.float32)
    for i in range(size):
        for j in range(i, size):
            entry = jnp.concatenate([factor[i, j]] * 2, axis=0) * scale
            upper = jnp.where((wide == j) & (tall == i), entry, upper)
    upper_ref[...] = upper[:size, :size]


def body(operator, adjacency, counts, rhs, start, shifts):
    elems, width, columns = operator.shape
    steps = shifts.shape[0]
    devices = lax.axis_size(AXES)
    packed = elems * width // LANES
    block = elems * ROWS + 2 * packed
    vmem = pl.BlockSpec(memory_space=pltpu.VMEM)
    smem = pl.BlockSpec(memory_space=pltpu.SMEM)
    hbm = pl.BlockSpec(memory_space=pl.ANY)
    mebi = 1024 * 1024
    f32 = jnp.float32

    x = start.reshape(packed, LANES)
    b = rhs.reshape(packed, LANES)
    own = pl.pallas_call(
        band_kernel,
        out_shape=jax.ShapeDtypeStruct((block, LANES), f32),
        in_specs=[hbm, smem, smem, hbm, hbm],
        out_specs=hbm,
        scratch_shapes=[
            pltpu.VMEM(operator.shape, f32),
            pltpu.VMEM((elems * ROWS, LANES), f32),
            pltpu.SemaphoreType.DMA((elems // CHUNK,)),
            pltpu.SemaphoreType.DMA((elems // CHUNK + 2,)),
        ],
        compiler_params=pltpu.CompilerParams(vmem_limit_bytes=60 * mebi),
        name="bands",
    )(operator, adjacency.T, counts, x, b)
    below = shifted(own, 1)
    above = shifted(own, -1)
    far_low = shifted(x[packed - 1 :], 2)
    far_high = shifted(x[:1], -2)
    basis, gram = pl.pallas_call(
        functools.partial(basis_kernel, elems, steps),
        out_shape=(
            jax.ShapeDtypeStruct((8 * (steps + 1), LANES), f32),
            jax.ShapeDtypeStruct((1, LANES), f32),
        ),
        in_specs=[vmem, vmem, vmem, vmem, vmem, smem],
        out_specs=(vmem, vmem),
        scratch_shapes=[pltpu.VMEM(((steps + 3) * (3 * elems + 2 * PAD), LANES), f32)],
        compiler_params=pltpu.CompilerParams(vmem_limit_bytes=16 * mebi),
        name="basis",
    )(below, own, above, far_low, far_high, shifts)
    gram = lax.psum(gram, AXES)
    sol, res, upper = pl.pallas_call(
        functools.partial(finish_kernel, devices * elems * width, steps),
        out_shape=(
            jax.ShapeDtypeStruct((packed, LANES), f32),
            jax.ShapeDtypeStruct((packed, LANES), f32),
            jax.ShapeDtypeStruct((steps + 1, steps + 1), f32),
        ),
        in_specs=[vmem, vmem, vmem, smem],
        out_specs=(vmem, vmem, vmem),
        compiler_params=pltpu.CompilerParams(vmem_limit_bytes=4 * mebi),
        name="finish",
    )(gram, basis, x, shifts)
    return (sol.reshape(-1), res.reshape(-1), upper)


def solution(mesh):
    split = P(AXES)
    return jax.shard_map(
        body,
        mesh=mesh,
        in_specs=(P(AXES, None, None), P(AXES, None), split, split, split, P()),
        out_specs=(split, split, P()),
        check_vma=False,
    )
```

```python
import functools

import jax
import jax.numpy as jnp
from jax import lax
from jax.experimental import pallas as pl
from jax.experimental.pallas import tpu as pltpu
from jax.sharding import PartitionSpec as P

AXES = ("group", "slab")
WIDTH = 64
LANES = 128
REACH = 2
BANDS = 2 * REACH + 1
HALF = WIDTH // 2
ROWS = BANDS * HALF
CHUNK = 4
PAD = 8


def shifted(array, by):
    size = lax.axis_size(AXES)
    pairs = [(i, i + by) for i in range(size) if 0 <= i + by < size]
    return lax.ppermute(array, AXES, pairs)


def between_chips(array):
    size = lax.axis_size(AXES)
    pairs = [(i, i + 1 if i % 2 else i - 1) for i in range(1, size - 1)]
    return lax.ppermute(array, AXES, pairs)


def within_chip(array):
    size = lax.axis_size(AXES)
    return lax.ppermute(array, AXES, [(i, i + 1 - 2 * (i % 2)) for i in range(size)])


def lane_ids(rows):
    return lax.broadcasted_iota(jnp.int32, (rows, LANES), 1)


def band_kernel(
    op_ref, adjacency_ref, valid_ref, start_ref, rhs_ref, out_ref,
    held, adj_ref, counts_ref, in_sems, out_sems,
):
    elems, _, columns = op_ref.shape
    faces = columns // WIDTH - 1
    chunks = elems // CHUNK
    base = lax.axis_index(AXES) * elems
    left = lane_ids(HALF) < WIDTH
    tail = elems * ROWS

    def arriving(chunk):
        part = pl.ds(chunk * CHUNK, CHUNK)
        return pltpu.make_async_copy(op_ref.at[part], held.at[part], in_sems.at[chunk])

    for chunk in range(chunks):
        arriving(chunk).start()
    scalars = [
        pltpu.make_async_copy(adjacency_ref, adj_ref, out_sems.at[0]),
        pltpu.make_async_copy(valid_ref, counts_ref, out_sems.at[1]),
    ]
    extras = [
        pltpu.make_async_copy(start_ref, out_ref.at[pl.ds(tail, 8), :], out_sems.at[2]),
        pltpu.make_async_copy(rhs_ref, out_ref.at[pl.ds(tail + 8, 8), :], out_sems.at[3]),
    ]
    for copy in scalars + extras:
        copy.start()
    for copy in scalars:
        copy.wait()

    def one(e):
        blocks = []
        for tile in range(columns // LANES):
            lanes = pl.ds(tile * LANES, LANES)
            top = held[e, pl.ds(0, HALF), lanes]
            low = held[e, pl.ds(HALF, HALF), lanes]
            blocks.append(jnp.where(left, top, pltpu.roll(low, WIDTH, 1)))
            blocks.append(jnp.where(left, pltpu.roll(top, WIDTH, 1), low))
        if columns % LANES:
            lanes = pl.ds(columns - WIDTH, WIDTH)
            top = held[e, pl.ds(0, HALF), lanes]
            low = held[e, pl.ds(HALF, HALF), lanes]
            blocks.append(jnp.concatenate([top, low], axis=1))
        count = counts_ref[e]
        place = []
        for face in range(faces):
            offset = adj_ref[face, e] - (base + e) + REACH
            place.append(jnp.where(face < count, offset, -1))
        for band in range(BANDS):
            rows = pl.ds(pl.multiple_of(e * ROWS + band * HALF, HALF), HALF)
            total = blocks[0] if band == REACH else None
            if band != REACH:
                for face in range(faces):
                    weight = jnp.where(place[face] == band, jnp.float32(1), jnp.float32(0))
                    term = blocks[face + 1] * weight
                    total = term if total is None else total + term
            out_ref[rows, :] = total

    def some(chunk, carry):
        arriving(chunk).wait()
        for k in range(CHUNK):
            one(chunk * CHUNK + k)
        return carry

    lax.fori_loop(0, chunks, some, 0)
    for extra in extras:
        extra.wait()


def stacked_sums(terms, row):
    for span in (4, 2, 1):
        low = (row & span) == 0
        half = len(terms) // 2
        merged = []
        for a, b in zip(terms[:half], terms[half:]):
            kept = jnp.where(low, a, b)
            if span == 4:
                moved = pltpu.roll(jnp.where(low, b, a), 4, 0)
            else:
                moved = jnp.where(low, pltpu.roll(a, 8 - span, 0), pltpu.roll(b, span, 0))
            merged.append(kept + moved)
        terms = merged
    return terms[0]


def basis_kernel(
    elems, steps,
    inner_ref, own_ref, outer_ref, far_low_ref, far_high_ref, shifts_ref,
    basis_ref, gram_ref,
    vecs,
):
    level = 3 * elems + 2 * PAD
    given = (steps + 2) * level
    lane = lane_ids(8)
    row = lax.broadcasted_iota(jnp.int32, (8, LANES), 0)
    left = lane < WIDTH
    half = lane_ids(HALF)
    left_half = half < WIDTH
    pick_top = half % WIDTH == lax.broadcasted_iota(jnp.int32, (HALF, LANES), 0)
    pick_low = half % WIDTH == lax.broadcasted_iota(jnp.int32, (HALF, LANES), 0) + HALF

    empty = jnp.zeros((8, LANES), jnp.float32)
    for at in range(0, vecs.shape[0], 8):
        vecs[pl.ds(at, 8), :] = empty

    def spread(at, packed):
        turned = pltpu.roll(packed, WIDTH, 1)
        vecs[pl.ds(at, 8, stride=2), :] = jnp.where(left, packed, turned)
        vecs[pl.ds(at + 1, 8, stride=2), :] = jnp.where(left, turned, packed)

    for ref, at in ((far_low_ref, PAD - 2), (far_high_ref, PAD + 3 * elems)):
        packed = jnp.broadcast_to(ref[...], (8, LANES))
        turned = pltpu.roll(packed, WIDTH, 1)
        vecs[pl.ds(at, 1), :] = jnp.where(left, packed, turned)[:1]
        vecs[pl.ds(at + 1, 1), :] = jnp.where(left, turned, packed)[:1]

    def fill(refs):
        tail = elems * ROWS
        for part, ref in enumerate(refs):
            spread(PAD + part * elems, ref[pl.ds(tail, 8), :])
            spread(given + PAD + part * elems, ref[pl.ds(tail + 8, 8), :])

        def times(part, first, at):
            near = [vecs[pl.ds(at + (k - REACH), 1), :] for k in range(8 + 2 * REACH)]
            terms = []
            for k in range(8):
                total = None
                for band in range(BANDS):
                    rows = pl.ds((first + k) * ROWS + band * HALF, HALF)
                    term = refs[part][rows, :] * near[k + band]
                    total = term if total is None else total + term
                top = jnp.sum(jnp.where(left_half, total, 0.0), axis=1, keepdims=True)
                low = jnp.sum(jnp.where(left_half, 0.0, total), axis=1, keepdims=True)
                placed = jnp.where(pick_top, top, jnp.where(pick_low, low, 0.0))
                terms.append(jnp.sum(placed.reshape(HALF // 8, 8, LANES), axis=0))
            return stacked_sums(terms, row)

        def apply(index, groups):
            at = pl.multiple_of(index * level + PAD, 8)
            if isinstance(index, int):
                opening = index == 0
                source = given + PAD if opening else at
                sign, scale = (-1.0, 1.0) if opening else (1.0, -shifts_ref[index - 1])
            else:
                opening = index == 0
                source = pl.multiple_of(jnp.where(opening, given + PAD, at), 8)
                sign = jnp.where(opening, jnp.float32(-1), jnp.float32(1))
                scale = jnp.where(opening, jnp.float32(1), -shifts_ref[jnp.maximum(index - 1, 0)])
            made = []
            for part, first in groups:
                place = part * elems + first
                fresh = times(part, first, at + place)
                made.append((place, sign * fresh + scale * vecs[pl.ds(source + place, 8), :]))
            for place, value in made:
                vecs[pl.ds(at + level + place, 8), :] = value

        own = [(1, first) for first in range(0, elems, 8)]
        groups = [(part, first) for part in (0, 2) for first in range(0, elems, 8)]
        done = 0
        while done <= steps:
            reach = REACH * (steps - done)
            wanted = [
                (part, first)
                for part, first in groups
                if (elems - first - 8 < reach if part == 0 else first < reach)
            ]
            until = done
            while until <= steps:
                later = REACH * (steps - until)
                if wanted != [
                    (part, first)
                    for part, first in groups
                    if (elems - first - 8 < later if part == 0 else first < later)
                ]:
                    break
                until += 1

            def turn(index, carry, wanted=wanted):
                apply(index, wanted + own)
                return carry

            if until - done == 1:
                apply(done, wanted + own)
            else:
                lax.fori_loop(done, until, turn, 0)
            done = until

    second = lax.axis_index(AXES) % 2 == 1

    @pl.when(second)
    def _():
        fill((inner_ref, own_ref, outer_ref))

    @pl.when(jnp.logical_not(second))
    def _():
        fill((outer_ref, own_ref, inner_ref))

    rows = []
    for k in range(steps + 1):
        at = (k + 1) * level + PAD + elems
        packed = jnp.where(left, vecs[pl.ds(at, 8, stride=2), :], vecs[pl.ds(at + 1, 8, stride=2), :])
        basis_ref[pl.ds(8 * k, 8), :] = packed
        rows.append(packed)
    total = jnp.zeros((8, LANES), jnp.float32)
    number = 0
    for i in range(steps + 1):
        for j in range(i, steps + 1):
            entry = jnp.sum(rows[i] * rows[j], axis=1, keepdims=True)
            total = jnp.where(lane == number, entry, total)
            number += 1
    gram = jnp.sum(total, axis=0, keepdims=True)
    gram_ref[...] = jnp.broadcast_to(gram, gram_ref.shape)


def inverse_root(value):
    guess = lax.rsqrt(value)
    return guess * (1.5 - 0.5 * value * guess * guess)


def finish_kernel(count, steps, parts_ref, basis_ref, start_ref, shifts_ref, sol_ref, res_ref, upper_ref):
    size = steps + 1
    lane = lane_ids(8)
    summed = jnp.broadcast_to(jnp.sum(parts_ref[...], axis=0, keepdims=True), (8, LANES))
    gram = {}
    number = 0
    for i in range(size):
        for j in range(i, size):
            entry = jnp.sum(jnp.where(lane == number, summed, 0.0), axis=1, keepdims=True)
            gram[i, j] = jnp.broadcast_to(entry, (8, LANES))
            number += 1
    factor = {}
    for k in range(size):
        turn = inverse_root(gram[k, k])
        for j in range(k, size):
            factor[k, j] = gram[k, j] * turn
        for i in range(k + 1, size):
            for j in range(i, size):
                gram[i, j] = gram[i, j] - factor[k, i] * factor[k, j]
    hess = {}
    for k in range(steps):
        for i in range(k + 1):
            hess[i, k] = factor[i, k] * shifts_ref[k] + factor[i, k + 1]
        hess[k + 1, k] = factor[k + 1, k + 1]
    target = [factor[0, 0]] + [jnp.zeros((8, LANES), jnp.float32)] * steps
    inverse = []
    for k in range(steps):
        a, b = hess[k, k], hess[k + 1, k]
        scale = inverse_root(a * a + b * b)
        cos, sin = a * scale, b * scale
        inverse.append(scale)
        for j in range(k + 1, steps):
            up, down = hess[k, j], hess[k + 1, j]
            hess[k, j] = cos * up + sin * down
            hess[k + 1, j] = cos * down - sin * up
        target[k], target[k + 1] = cos * target[k], -(sin * target[k])
    coeffs = [None] * steps
    for k in range(steps - 1, -1, -1):
        value = target[k]
        for j in range(k + 1, steps):
            value = value - hess[k, j] * coeffs[j]
        coeffs[k] = value * inverse[k]
    rows = [basis_ref[pl.ds(8 * k, 8), :] for k in range(size)]
    sol, res = 0.0, 0.0
    for k in range(steps):
        sol = sol + coeffs[k] * rows[k]
        res = res + coeffs[k] * (rows[k + 1] + shifts_ref[k] * rows[k])
    sol_ref[...] = start_ref[...] + sol
    res_ref[...] = rows[0] - res
    wide = lane_ids(16)
    tall = lax.broadcasted_iota(jnp.int32, (16, LANES), 0)
    scale = 1.0 / (count ** 0.5)
    upper = jnp.zeros((16, LANES), jnp.float32)
    for i in range(size):
        for j in range(i, size):
            entry = jnp.concatenate([factor[i, j]] * 2, axis=0) * scale
            upper = jnp.where((wide == j) & (tall == i), entry, upper)
    upper_ref[...] = upper[:size, :size]


def body(operator, adjacency, counts, rhs, start, shifts):
    elems, width, columns = operator.shape
    steps = shifts.shape[0]
    devices = lax.axis_size(AXES)
    packed = elems * width // LANES
    block = elems * ROWS + 2 * packed
    vmem = pl.BlockSpec(memory_space=pltpu.VMEM)
    smem = pl.BlockSpec(memory_space=pltpu.SMEM)
    hbm = pl.BlockSpec(memory_space=pl.ANY)
    mebi = 1024 * 1024
    f32 = jnp.float32

    x = start.reshape(packed, LANES)
    b = rhs.reshape(packed, LANES)
    sources = (operator, adjacency.T, counts, x, b)
    own = pl.pallas_call(
        band_kernel,
        out_shape=pltpu.VMEM((block, LANES), f32),
        in_specs=[hbm] * 5,
        out_specs=vmem,
        scratch_shapes=[
            pltpu.VMEM(operator.shape, f32),
            pltpu.SMEM(adjacency.T.shape, jnp.int32),
            pltpu.SMEM(counts.shape, jnp.int32),
            pltpu.SemaphoreType.DMA((elems // CHUNK,)),
            pltpu.SemaphoreType.DMA((4,)),
        ],
        compiler_params=pltpu.CompilerParams(vmem_limit_bytes=16 * mebi),
        name="bands",
    )(*(pltpu.with_memory_space_constraint(source, pltpu.HBM) for source in sources))
    inner = within_chip(own)
    outer = between_chips(own)
    far_low = shifted(x[packed - 1 :], 2)
    far_high = shifted(x[:1], -2)
    basis, gram = pl.pallas_call(
        functools.partial(basis_kernel, elems, steps),
        out_shape=(
            jax.ShapeDtypeStruct((8 * (steps + 1), LANES), f32),
            jax.ShapeDtypeStruct((devices, LANES), f32),
        ),
        in_specs=[vmem, vmem, vmem, vmem, vmem, smem],
        out_specs=(vmem, vmem),
        scratch_shapes=[pltpu.VMEM(((steps + 3) * (3 * elems + 2 * PAD), LANES), f32)],
        compiler_params=pltpu.CompilerParams(vmem_limit_bytes=16 * mebi),
        name="basis",
    )(inner, own, outer, far_low, far_high, shifts)
    parts = lax.all_to_all(gram, AXES, 0, 0, tiled=True)
    sol, res, upper = pl.pallas_call(
        functools.partial(finish_kernel, devices * elems * width, steps),
        out_shape=(
            jax.ShapeDtypeStruct((packed, LANES), f32),
            jax.ShapeDtypeStruct((packed, LANES), f32),
            jax.ShapeDtypeStruct((steps + 1, steps + 1), f32),
        ),
        in_specs=[vmem, vmem, vmem, smem],
        out_specs=(vmem, vmem, vmem),
        compiler_params=pltpu.CompilerParams(vmem_limit_bytes=4 * mebi),
        name="finish",
    )(parts, basis, x, shifts)
    return (sol.reshape(-1), res.reshape(-1), upper)


def solution(mesh):
    split = P(AXES)
    return jax.shard_map(
        body,
        mesh=mesh,
        in_specs=(P(AXES, None, None), P(AXES, None), split, split, split, P()),
        out_specs=(split, split, P()),
        check_vma=False,
    )
```

```python
import functools

import jax
import jax.numpy as jnp
from jax import lax
from jax.experimental import pallas as pl
from jax.experimental.pallas import tpu as pltpu
from jax.sharding import PartitionSpec as P

AXES = ("group", "slab")
WIDTH = 64
LANES = 128
REACH = 2
BANDS = 2 * REACH + 1
HALF = WIDTH // 2
ROWS = BANDS * HALF
CHUNK = 4
PAD = 8


def shifted(array, by):
    size = lax.axis_size(AXES)
    pairs = [(i, i + by) for i in range(size) if 0 <= i + by < size]
    return lax.ppermute(array, AXES, pairs)


def between_chips(array):
    size = lax.axis_size(AXES)
    pairs = [(i, i + 1 if i % 2 else i - 1) for i in range(1, size - 1)]
    return lax.ppermute(array, AXES, pairs)


def within_chip(array):
    size = lax.axis_size(AXES)
    return lax.ppermute(array, AXES, [(i, i + 1 - 2 * (i % 2)) for i in range(size)])


def lane_ids(rows):
    return lax.broadcasted_iota(jnp.int32, (rows, LANES), 1)


def band_kernel(
    op_ref, adjacency_ref, valid_ref, start_ref, rhs_ref, out_ref,
    held, adj_ref, counts_ref, in_sems, out_sems,
):
    elems, _, columns = op_ref.shape
    faces = columns // WIDTH - 1
    chunks = elems // CHUNK
    base = lax.axis_index(AXES) * elems
    left = lane_ids(HALF) < WIDTH
    tail = elems * ROWS

    def arriving(chunk):
        part = pl.ds(chunk * CHUNK, CHUNK)
        return pltpu.make_async_copy(op_ref.at[part], held.at[part], in_sems.at[chunk])

    for chunk in range(chunks):
        arriving(chunk).start()
    scalars = [
        pltpu.make_async_copy(adjacency_ref, adj_ref, out_sems.at[0]),
        pltpu.make_async_copy(valid_ref, counts_ref, out_sems.at[1]),
    ]
    extras = [
        pltpu.make_async_copy(start_ref, out_ref.at[pl.ds(tail, 8), :], out_sems.at[2]),
        pltpu.make_async_copy(rhs_ref, out_ref.at[pl.ds(tail + 8, 8), :], out_sems.at[3]),
    ]
    for copy in scalars + extras:
        copy.start()
    for copy in scalars:
        copy.wait()

    def one(e):
        blocks = []
        for tile in range(columns // LANES):
            lanes = pl.ds(tile * LANES, LANES)
            top = held[e, pl.ds(0, HALF), lanes]
            low = held[e, pl.ds(HALF, HALF), lanes]
            blocks.append(jnp.where(left, top, pltpu.roll(low, WIDTH, 1)))
            blocks.append(jnp.where(left, pltpu.roll(top, WIDTH, 1), low))
        if columns % LANES:
            lanes = pl.ds(columns - WIDTH, WIDTH)
            top = held[e, pl.ds(0, HALF), lanes]
            low = held[e, pl.ds(HALF, HALF), lanes]
            blocks.append(jnp.concatenate([top, low], axis=1))
        count = counts_ref[e]
        place = []
        for face in range(faces):
            offset = adj_ref[face, e] - (base + e) + REACH
            place.append(jnp.where(face < count, offset, -1))
        for band in range(BANDS):
            rows = pl.ds(pl.multiple_of(e * ROWS + band * HALF, HALF), HALF)
            total = blocks[0] if band == REACH else None
            if band != REACH:
                for face in range(faces):
                    weight = jnp.where(place[face] == band, jnp.float32(1), jnp.float32(0))
                    term = blocks[face + 1] * weight
                    total = term if total is None else total + term
            out_ref[rows, :] = total

    def some(chunk, carry):
        arriving(chunk).wait()
        for k in range(CHUNK):
            one(chunk * CHUNK + k)
        return carry

    lax.fori_loop(0, chunks, some, 0)
    for extra in extras:
        extra.wait()


def stacked_sums(terms, row):
    for span in (4, 2, 1):
        low = (row & span) == 0
        half = len(terms) // 2
        merged = []
        for a, b in zip(terms[:half], terms[half:]):
            kept = jnp.where(low, a, b)
            if span == 4:
                moved = pltpu.roll(jnp.where(low, b, a), 4, 0)
            else:
                moved = jnp.where(low, pltpu.roll(a, 8 - span, 0), pltpu.roll(b, span, 0))
            merged.append(kept + moved)
        terms = merged
    return terms[0]


def basis_kernel(
    elems, steps,
    inner_ref, own_ref, outer_ref, far_low_ref, far_high_ref, shifts_ref,
    basis_ref, gram_ref,
    vecs,
):
    level = 3 * elems + 2 * PAD
    given = (steps + 2) * level
    lane = lane_ids(8)
    row = lax.broadcasted_iota(jnp.int32, (8, LANES), 0)
    left = lane < WIDTH
    half = lane_ids(HALF)
    left_half = half < WIDTH
    pick_top = half % WIDTH == lax.broadcasted_iota(jnp.int32, (HALF, LANES), 0)
    pick_low = half % WIDTH == lax.broadcasted_iota(jnp.int32, (HALF, LANES), 0) + HALF

    empty = jnp.zeros((8, LANES), jnp.float32)
    for at in range(0, vecs.shape[0], 8):
        vecs[pl.ds(at, 8), :] = empty

    def spread(at, packed):
        turned = pltpu.roll(packed, WIDTH, 1)
        vecs[pl.ds(at, 8, stride=2), :] = jnp.where(left, packed, turned)
        vecs[pl.ds(at + 1, 8, stride=2), :] = jnp.where(left, turned, packed)

    for ref, at in ((far_low_ref, PAD - 2), (far_high_ref, PAD + 3 * elems)):
        packed = jnp.broadcast_to(ref[...], (8, LANES))
        turned = pltpu.roll(packed, WIDTH, 1)
        vecs[pl.ds(at, 1), :] = jnp.where(left, packed, turned)[:1]
        vecs[pl.ds(at + 1, 1), :] = jnp.where(left, turned, packed)[:1]

    def fill(refs):
        tail = elems * ROWS
        for part, ref in enumerate(refs):
            spread(PAD + part * elems, ref[pl.ds(tail, 8), :])
            spread(given + PAD + part * elems, ref[pl.ds(tail + 8, 8), :])

        def times(part, first, at):
            near = [vecs[pl.ds(at + (k - REACH), 1), :] for k in range(8 + 2 * REACH)]
            terms = []
            for k in range(8):
                total = None
                for band in range(BANDS):
                    rows = pl.ds((first + k) * ROWS + band * HALF, HALF)
                    term = refs[part][rows, :] * near[k + band]
                    total = term if total is None else total + term
                top = jnp.sum(jnp.where(left_half, total, 0.0), axis=1, keepdims=True)
                low = jnp.sum(jnp.where(left_half, 0.0, total), axis=1, keepdims=True)
                placed = jnp.where(pick_top, top, jnp.where(pick_low, low, 0.0))
                terms.append(jnp.sum(placed.reshape(HALF // 8, 8, LANES), axis=0))
            return stacked_sums(terms, row)

        def apply(index, groups):
            at = pl.multiple_of(index * level + PAD, 8)
            if isinstance(index, int):
                opening = index == 0
                source = given + PAD if opening else at
                sign, scale = (-1.0, 1.0) if opening else (1.0, -shifts_ref[index - 1])
            else:
                opening = index == 0
                source = pl.multiple_of(jnp.where(opening, given + PAD, at), 8)
                sign = jnp.where(opening, jnp.float32(-1), jnp.float32(1))
                scale = jnp.where(opening, jnp.float32(1), -shifts_ref[jnp.maximum(index - 1, 0)])
            made = []
            for part, first in groups:
                place = part * elems + first
                fresh = times(part, first, at + place)
                made.append((place, sign * fresh + scale * vecs[pl.ds(source + place, 8), :]))
            for place, value in made:
                vecs[pl.ds(at + level + place, 8), :] = value

        own = [(1, first) for first in range(0, elems, 8)]
        groups = [(part, first) for part in (0, 2) for first in range(0, elems, 8)]
        done = 0
        while done <= steps:
            reach = REACH * (steps - done)
            wanted = [
                (part, first)
                for part, first in groups
                if (elems - first - 8 < reach if part == 0 else first < reach)
            ]
            until = done
            while until <= steps:
                later = REACH * (steps - until)
                if wanted != [
                    (part, first)
                    for part, first in groups
                    if (elems - first - 8 < later if part == 0 else first < later)
                ]:
                    break
                until += 1

            def turn(index, carry, wanted=wanted):
                apply(index, wanted + own)
                return carry

            if until - done == 1:
                apply(done, wanted + own)
            else:
                lax.fori_loop(done, until, turn, 0)
            done = until

    second = lax.axis_index(AXES) % 2 == 1

    @pl.when(second)
    def _():
        fill((inner_ref, own_ref, outer_ref))

    @pl.when(jnp.logical_not(second))
    def _():
        fill((outer_ref, own_ref, inner_ref))

    rows = []
    for k in range(steps + 1):
        at = (k + 1) * level + PAD + elems
        packed = jnp.where(left, vecs[pl.ds(at, 8, stride=2), :], vecs[pl.ds(at + 1, 8, stride=2), :])
        basis_ref[pl.ds(8 * k, 8), :] = packed
        rows.append(packed)
    total = jnp.zeros((8, LANES), jnp.float32)
    number = 0
    for i in range(steps + 1):
        for j in range(i, steps + 1):
            entry = jnp.sum(rows[i] * rows[j], axis=1, keepdims=True)
            total = jnp.where(lane == number, entry, total)
            number += 1
    gram = jnp.sum(total, axis=0, keepdims=True)
    gram_ref[...] = jnp.broadcast_to(gram, gram_ref.shape)


def partial_kernel(parts_ref, out_ref):
    total = jnp.sum(parts_ref[...], axis=0, keepdims=True)
    out_ref[...] = jnp.broadcast_to(total, out_ref.shape)


def inverse_root(value):
    guess = lax.rsqrt(value)
    return guess * (1.5 - 0.5 * value * guess * guess)


def finish_kernel(count, steps, parts_ref, basis_ref, start_ref, shifts_ref, sol_ref, res_ref, upper_ref):
    size = steps + 1
    lane = lane_ids(8)
    summed = jnp.broadcast_to(jnp.sum(parts_ref[...], axis=0, keepdims=True), (8, LANES))
    gram = {}
    number = 0
    for i in range(size):
        for j in range(i, size):
            entry = jnp.sum(jnp.where(lane == number, summed, 0.0), axis=1, keepdims=True)
            gram[i, j] = jnp.broadcast_to(entry, (8, LANES))
            number += 1
    factor = {}
    for k in range(size):
        turn = inverse_root(gram[k, k])
        for j in range(k, size):
            factor[k, j] = gram[k, j] * turn
        for i in range(k + 1, size):
            for j in range(i, size):
                gram[i, j] = gram[i, j] - factor[k, i] * factor[k, j]
    hess = {}
    for k in range(steps):
        for i in range(k + 1):
            hess[i, k] = factor[i, k] * shifts_ref[k] + factor[i, k + 1]
        hess[k + 1, k] = factor[k + 1, k + 1]
    target = [factor[0, 0]] + [jnp.zeros((8, LANES), jnp.float32)] * steps
    inverse = []
    for k in range(steps):
        a, b = hess[k, k], hess[k + 1, k]
        scale = inverse_root(a * a + b * b)
        cos, sin = a * scale, b * scale
        inverse.append(scale)
        for j in range(k + 1, steps):
            up, down = hess[k, j], hess[k + 1, j]
            hess[k, j] = cos * up + sin * down
            hess[k + 1, j] = cos * down - sin * up
        target[k], target[k + 1] = cos * target[k], -(sin * target[k])
    coeffs = [None] * steps
    for k in range(steps - 1, -1, -1):
        value = target[k]
        for j in range(k + 1, steps):
            value = value - hess[k, j] * coeffs[j]
        coeffs[k] = value * inverse[k]
    rows = [basis_ref[pl.ds(8 * k, 8), :] for k in range(size)]
    sol, res = 0.0, 0.0
    for k in range(steps):
        sol = sol + coeffs[k] * rows[k]
        res = res + coeffs[k] * (rows[k + 1] + shifts_ref[k] * rows[k])
    sol_ref[...] = start_ref[...] + sol
    res_ref[...] = rows[0] - res
    wide = lane_ids(16)
    tall = lax.broadcasted_iota(jnp.int32, (16, LANES), 0)
    scale = 1.0 / (count ** 0.5)
    upper = jnp.zeros((16, LANES), jnp.float32)
    for i in range(size):
        for j in range(i, size):
            entry = jnp.concatenate([factor[i, j]] * 2, axis=0) * scale
            upper = jnp.where((wide == j) & (tall == i), entry, upper)
    upper_ref[...] = upper[:size, :size]


def body(operator, adjacency, counts, rhs, start, shifts):
    elems, width, columns = operator.shape
    steps = shifts.shape[0]
    devices = lax.axis_size(AXES)
    slabs = lax.axis_size("slab")
    groups = lax.axis_size("group")
    packed = elems * width // LANES
    block = elems * ROWS + 2 * packed
    vmem = pl.BlockSpec(memory_space=pltpu.VMEM)
    smem = pl.BlockSpec(memory_space=pltpu.SMEM)
    hbm = pl.BlockSpec(memory_space=pl.ANY)
    mebi = 1024 * 1024
    f32 = jnp.float32

    x = start.reshape(packed, LANES)
    b = rhs.reshape(packed, LANES)
    sources = (operator, adjacency.T, counts, x, b)
    own = pl.pallas_call(
        band_kernel,
        out_shape=pltpu.VMEM((block, LANES), f32),
        in_specs=[hbm] * 5,
        out_specs=vmem,
        scratch_shapes=[
            pltpu.VMEM(operator.shape, f32),
            pltpu.SMEM(adjacency.T.shape, jnp.int32),
            pltpu.SMEM(counts.shape, jnp.int32),
            pltpu.SemaphoreType.DMA((elems // CHUNK,)),
            pltpu.SemaphoreType.DMA((4,)),
        ],
        compiler_params=pltpu.CompilerParams(vmem_limit_bytes=16 * mebi),
        name="bands",
    )(*(pltpu.with_memory_space_constraint(source, pltpu.HBM) for source in sources))
    inner = within_chip(own)
    outer = between_chips(own)
    far_low = shifted(x[packed - 1 :], 2)
    far_high = shifted(x[:1], -2)
    basis, gram = pl.pallas_call(
        functools.partial(basis_kernel, elems, steps),
        out_shape=(
            jax.ShapeDtypeStruct((8 * (steps + 1), LANES), f32),
            jax.ShapeDtypeStruct((slabs, LANES), f32),
        ),
        in_specs=[vmem, vmem, vmem, vmem, vmem, smem],
        out_specs=(vmem, vmem),
        scratch_shapes=[pltpu.VMEM(((steps + 3) * (3 * elems + 2 * PAD), LANES), f32)],
        compiler_params=pltpu.CompilerParams(vmem_limit_bytes=16 * mebi),
        name="basis",
    )(inner, own, outer, far_low, far_high, shifts)
    parts = lax.all_to_all(gram, "slab", 0, 0, tiled=True)
    parts = pl.pallas_call(
        partial_kernel,
        out_shape=jax.ShapeDtypeStruct((groups, LANES), f32),
        in_specs=[vmem],
        out_specs=vmem,
        compiler_params=pltpu.CompilerParams(vmem_limit_bytes=4 * mebi),
        name="partial",
    )(parts)
    parts = lax.all_to_all(parts, "group", 0, 0, tiled=True)
    sol, res, upper = pl.pallas_call(
        functools.partial(finish_kernel, devices * elems * width, steps),
        out_shape=(
            jax.ShapeDtypeStruct((packed, LANES), f32),
            jax.ShapeDtypeStruct((packed, LANES), f32),
            jax.ShapeDtypeStruct((steps + 1, steps + 1), f32),
        ),
        in_specs=[vmem, vmem, vmem, smem],
        out_specs=(vmem, vmem, vmem),
        compiler_params=pltpu.CompilerParams(vmem_limit_bytes=4 * mebi),
        name="finish",
    )(parts, basis, x, shifts)
    return (sol.reshape(-1), res.reshape(-1), upper)


def solution(mesh):
    split = P(AXES)
    return jax.shard_map(
        body,
        mesh=mesh,
        in_specs=(P(AXES, None, None), P(AXES, None), split, split, split, P()),
        out_specs=(split, split, P()),
        check_vma=False,
    )
```

```python
import functools

import jax
import jax.numpy as jnp
from jax import lax
from jax.experimental import pallas as pl
from jax.experimental.pallas import tpu as pltpu
from jax.sharding import PartitionSpec as P

AXES = ("group", "slab")
WIDTH = 64
LANES = 128
REACH = 2
BANDS = 2 * REACH + 1
HALF = WIDTH // 2
ROWS = BANDS * HALF
CHUNK = 4
PAD = 8


def shifted(array, by):
    size = lax.axis_size(AXES)
    pairs = [(i, i + by) for i in range(size) if 0 <= i + by < size]
    return lax.ppermute(array, AXES, pairs)


def between_chips(array):
    size = lax.axis_size(AXES)
    pairs = [(i, i + 1 if i % 2 else i - 1) for i in range(1, size - 1)]
    return lax.ppermute(array, AXES, pairs)


def within_chip(array):
    size = lax.axis_size(AXES)
    return lax.ppermute(array, AXES, [(i, i + 1 - 2 * (i % 2)) for i in range(size)])


def lane_ids(rows):
    return lax.broadcasted_iota(jnp.int32, (rows, LANES), 1)


def band_kernel(
    op_ref, adjacency_ref, valid_ref, start_ref, rhs_ref, out_ref,
    held, adj_ref, counts_ref, in_sems, out_sems,
):
    elems, _, columns = op_ref.shape
    faces = columns // WIDTH - 1
    chunks = elems // CHUNK
    base = lax.axis_index(AXES) * elems
    left = lane_ids(HALF) < WIDTH
    tail = elems * ROWS

    def arriving(chunk):
        part = pl.ds(chunk * CHUNK, CHUNK)
        return pltpu.make_async_copy(op_ref.at[part], held.at[part], in_sems.at[chunk])

    for chunk in range(chunks):
        arriving(chunk).start()
    scalars = [
        pltpu.make_async_copy(adjacency_ref, adj_ref, out_sems.at[0]),
        pltpu.make_async_copy(valid_ref, counts_ref, out_sems.at[1]),
    ]
    extras = [
        pltpu.make_async_copy(start_ref, out_ref.at[pl.ds(tail, 8), :], out_sems.at[2]),
        pltpu.make_async_copy(rhs_ref, out_ref.at[pl.ds(tail + 8, 8), :], out_sems.at[3]),
    ]
    for copy in scalars + extras:
        copy.start()
    for copy in scalars:
        copy.wait()

    def one(e):
        blocks = []
        for tile in range(columns // LANES):
            lanes = pl.ds(tile * LANES, LANES)
            top = held[e, pl.ds(0, HALF), lanes]
            low = held[e, pl.ds(HALF, HALF), lanes]
            blocks.append(jnp.where(left, top, pltpu.roll(low, WIDTH, 1)))
            blocks.append(jnp.where(left, pltpu.roll(top, WIDTH, 1), low))
        if columns % LANES:
            lanes = pl.ds(columns - WIDTH, WIDTH)
            top = held[e, pl.ds(0, HALF), lanes]
            low = held[e, pl.ds(HALF, HALF), lanes]
            blocks.append(jnp.concatenate([top, low], axis=1))
        count = counts_ref[e]
        place = []
        for face in range(faces):
            offset = adj_ref[face, e] - (base + e) + REACH
            place.append(jnp.where(face < count, offset, -1))
        for band in range(BANDS):
            rows = pl.ds(pl.multiple_of(e * ROWS + band * HALF, HALF), HALF)
            total = blocks[0] if band == REACH else None
            if band != REACH:
                for face in range(faces):
                    weight = jnp.where(place[face] == band, jnp.float32(1), jnp.float32(0))
                    term = blocks[face + 1] * weight
                    total = term if total is None else total + term
            out_ref[rows, :] = total

    def some(chunk, carry):
        arriving(chunk).wait()
        for k in range(CHUNK):
            one(chunk * CHUNK + k)
        return carry

    lax.fori_loop(0, chunks, some, 0)
    for extra in extras:
        extra.wait()


def stacked_sums(terms, row):
    for span in (4, 2, 1):
        low = (row & span) == 0
        half = len(terms) // 2
        merged = []
        for a, b in zip(terms[:half], terms[half:]):
            kept = jnp.where(low, a, b)
            if span == 4:
                moved = pltpu.roll(jnp.where(low, b, a), 4, 0)
            else:
                moved = jnp.where(low, pltpu.roll(a, 8 - span, 0), pltpu.roll(b, span, 0))
            merged.append(kept + moved)
        terms = merged
    return terms[0]


def basis_kernel(
    elems, steps,
    inner_ref, own_ref, outer_ref, far_low_ref, far_high_ref, shifts_ref,
    basis_ref, gram_ref,
    vecs,
):
    level = 3 * elems + 2 * PAD
    given = (steps + 2) * level
    lane = lane_ids(8)
    row = lax.broadcasted_iota(jnp.int32, (8, LANES), 0)
    left = lane < WIDTH
    half = lane_ids(HALF)
    left_half = half < WIDTH
    pick_top = half % WIDTH == lax.broadcasted_iota(jnp.int32, (HALF, LANES), 0)
    pick_low = half % WIDTH == lax.broadcasted_iota(jnp.int32, (HALF, LANES), 0) + HALF

    empty = jnp.zeros((8, LANES), jnp.float32)
    for at in range(0, vecs.shape[0], 8):
        vecs[pl.ds(at, 8), :] = empty

    def spread(at, packed):
        turned = pltpu.roll(packed, WIDTH, 1)
        vecs[pl.ds(at, 8, stride=2), :] = jnp.where(left, packed, turned)
        vecs[pl.ds(at + 1, 8, stride=2), :] = jnp.where(left, turned, packed)

    for ref, at in ((far_low_ref, PAD - 2), (far_high_ref, PAD + 3 * elems)):
        packed = jnp.broadcast_to(ref[...], (8, LANES))
        turned = pltpu.roll(packed, WIDTH, 1)
        vecs[pl.ds(at, 1), :] = jnp.where(left, packed, turned)[:1]
        vecs[pl.ds(at + 1, 1), :] = jnp.where(left, turned, packed)[:1]

    def fill(refs):
        tail = elems * ROWS
        for part, ref in enumerate(refs):
            spread(PAD + part * elems, ref[pl.ds(tail, 8), :])
            spread(given + PAD + part * elems, ref[pl.ds(tail + 8, 8), :])

        def times(part, first, at):
            near = [vecs[pl.ds(at + (k - REACH), 1), :] for k in range(8 + 2 * REACH)]
            terms = []
            for k in range(8):
                total = None
                for band in range(BANDS):
                    rows = pl.ds((first + k) * ROWS + band * HALF, HALF)
                    term = refs[part][rows, :] * near[k + band]
                    total = term if total is None else total + term
                top = jnp.sum(jnp.where(left_half, total, 0.0), axis=1, keepdims=True)
                low = jnp.sum(jnp.where(left_half, 0.0, total), axis=1, keepdims=True)
                placed = jnp.where(pick_top, top, jnp.where(pick_low, low, 0.0))
                terms.append(jnp.sum(placed.reshape(HALF // 8, 8, LANES), axis=0))
            return stacked_sums(terms, row)

        def apply(index, groups):
            at = pl.multiple_of(index * level + PAD, 8)
            if isinstance(index, int):
                opening = index == 0
                source = given + PAD if opening else at
                sign, scale = (-1.0, 1.0) if opening else (1.0, -shifts_ref[index - 1])
            else:
                opening = index == 0
                source = pl.multiple_of(jnp.where(opening, given + PAD, at), 8)
                sign = jnp.where(opening, jnp.float32(-1), jnp.float32(1))
                scale = jnp.where(opening, jnp.float32(1), -shifts_ref[jnp.maximum(index - 1, 0)])
            made = []
            for part, first in groups:
                place = part * elems + first
                fresh = times(part, first, at + place)
                made.append((place, sign * fresh + scale * vecs[pl.ds(source + place, 8), :]))
            for place, value in made:
                vecs[pl.ds(at + level + place, 8), :] = value

        own = [(1, first) for first in range(0, elems, 8)]
        groups = [(part, first) for part in (0, 2) for first in range(0, elems, 8)]
        done = 0
        while done <= steps:
            reach = REACH * (steps - done)
            wanted = [
                (part, first)
                for part, first in groups
                if (elems - first - 8 < reach if part == 0 else first < reach)
            ]
            until = done
            while until <= steps:
                later = REACH * (steps - until)
                if wanted != [
                    (part, first)
                    for part, first in groups
                    if (elems - first - 8 < later if part == 0 else first < later)
                ]:
                    break
                until += 1

            def turn(index, carry, wanted=wanted):
                apply(index, wanted + own)
                return carry

            if until - done == 1:
                apply(done, wanted + own)
            else:
                lax.fori_loop(done, until, turn, 0)
            done = until

    second = lax.axis_index(AXES) % 2 == 1

    @pl.when(second)
    def _():
        fill((inner_ref, own_ref, outer_ref))

    @pl.when(jnp.logical_not(second))
    def _():
        fill((outer_ref, own_ref, inner_ref))

    rows = []
    for k in range(steps + 1):
        at = (k + 1) * level + PAD + elems
        packed = jnp.where(left, vecs[pl.ds(at, 8, stride=2), :], vecs[pl.ds(at + 1, 8, stride=2), :])
        basis_ref[pl.ds(8 * k, 8), :] = packed
        rows.append(packed)
    total = jnp.zeros((8, LANES), jnp.float32)
    number = 0
    for i in range(steps + 1):
        for j in range(i, steps + 1):
            entry = jnp.sum(rows[i] * rows[j], axis=1, keepdims=True)
            total = jnp.where(lane == number, entry, total)
            number += 1
    gram_ref[...] = jnp.sum(total, axis=0, keepdims=True)


def inverse_root(value):
    guess = lax.rsqrt(value)
    return guess * (1.5 - 0.5 * value * guess * guess)


def finish_kernel(count, steps, parts_ref, basis_ref, start_ref, shifts_ref, sol_ref, res_ref, upper_ref):
    size = steps + 1
    lane = lane_ids(8)
    summed = jnp.broadcast_to(jnp.sum(parts_ref[...], axis=0, keepdims=True), (8, LANES))
    gram = {}
    number = 0
    for i in range(size):
        for j in range(i, size):
            entry = jnp.sum(jnp.where(lane == number, summed, 0.0), axis=1, keepdims=True)
            gram[i, j] = jnp.broadcast_to(entry, (8, LANES))
            number += 1
    factor = {}
    for k in range(size):
        turn = inverse_root(gram[k, k])
        for j in range(k, size):
            factor[k, j] = gram[k, j] * turn
        for i in range(k + 1, size):
            for j in range(i, size):
                gram[i, j] = gram[i, j] - factor[k, i] * factor[k, j]
    hess = {}
    for k in range(steps):
        for i in range(k + 1):
            hess[i, k] = factor[i, k] * shifts_ref[k] + factor[i, k + 1]
        hess[k + 1, k] = factor[k + 1, k + 1]
    target = [factor[0, 0]] + [jnp.zeros((8, LANES), jnp.float32)] * steps
    inverse = []
    for k in range(steps):
        a, b = hess[k, k], hess[k + 1, k]
        scale = inverse_root(a * a + b * b)
        cos, sin = a * scale, b * scale
        inverse.append(scale)
        for j in range(k + 1, steps):
            up, down = hess[k, j], hess[k + 1, j]
            hess[k, j] = cos * up + sin * down
            hess[k + 1, j] = cos * down - sin * up
        target[k], target[k + 1] = cos * target[k], -(sin * target[k])
    coeffs = [None] * steps
    for k in range(steps - 1, -1, -1):
        value = target[k]
        for j in range(k + 1, steps):
            value = value - hess[k, j] * coeffs[j]
        coeffs[k] = value * inverse[k]
    rows = [basis_ref[pl.ds(8 * k, 8), :] for k in range(size)]
    sol, res = 0.0, 0.0
    for k in range(steps):
        sol = sol + coeffs[k] * rows[k]
        res = res + coeffs[k] * (rows[k + 1] + shifts_ref[k] * rows[k])
    sol_ref[...] = start_ref[...] + sol
    res_ref[...] = rows[0] - res
    wide = lane_ids(16)
    tall = lax.broadcasted_iota(jnp.int32, (16, LANES), 0)
    scale = 1.0 / (count ** 0.5)
    upper = jnp.zeros((16, LANES), jnp.float32)
    for i in range(size):
        for j in range(i, size):
            entry = jnp.concatenate([factor[i, j]] * 2, axis=0) * scale
            upper = jnp.where((wide == j) & (tall == i), entry, upper)
    upper_ref[...] = upper[:size, :size]


def body(operator, adjacency, counts, rhs, start, shifts):
    elems, width, columns = operator.shape
    steps = shifts.shape[0]
    devices = lax.axis_size(AXES)
    packed = elems * width // LANES
    block = elems * ROWS + 2 * packed
    vmem = pl.BlockSpec(memory_space=pltpu.VMEM)
    smem = pl.BlockSpec(memory_space=pltpu.SMEM)
    hbm = pl.BlockSpec(memory_space=pl.ANY)
    mebi = 1024 * 1024
    f32 = jnp.float32

    x = start.reshape(packed, LANES)
    b = rhs.reshape(packed, LANES)
    sources = (operator, adjacency.T, counts, x, b)
    own = pl.pallas_call(
        band_kernel,
        out_shape=pltpu.VMEM((block, LANES), f32),
        in_specs=[hbm] * 5,
        out_specs=vmem,
        scratch_shapes=[
            pltpu.VMEM(operator.shape, f32),
            pltpu.SMEM(adjacency.T.shape, jnp.int32),
            pltpu.SMEM(counts.shape, jnp.int32),
            pltpu.SemaphoreType.DMA((elems // CHUNK,)),
            pltpu.SemaphoreType.DMA((4,)),
        ],
        compiler_params=pltpu.CompilerParams(vmem_limit_bytes=16 * mebi),
        name="bands",
    )(*(pltpu.with_memory_space_constraint(source, pltpu.HBM) for source in sources))
    inner = within_chip(own)
    outer = between_chips(own)
    far_low = shifted(x[packed - 1 :], 2)
    far_high = shifted(x[:1], -2)
    basis, gram = pl.pallas_call(
        functools.partial(basis_kernel, elems, steps),
        out_shape=(
            jax.ShapeDtypeStruct((8 * (steps + 1), LANES), f32),
            jax.ShapeDtypeStruct((1, LANES), f32),
        ),
        in_specs=[vmem, vmem, vmem, vmem, vmem, smem],
        out_specs=(vmem, vmem),
        scratch_shapes=[pltpu.VMEM(((steps + 3) * (3 * elems + 2 * PAD), LANES), f32)],
        compiler_params=pltpu.CompilerParams(vmem_limit_bytes=16 * mebi),
        name="basis",
    )(inner, own, outer, far_low, far_high, shifts)
    parts = lax.all_gather(gram, AXES, axis=0, tiled=True)
    sol, res, upper = pl.pallas_call(
        functools.partial(finish_kernel, devices * elems * width, steps),
        out_shape=(
            jax.ShapeDtypeStruct((packed, LANES), f32),
            jax.ShapeDtypeStruct((packed, LANES), f32),
            jax.ShapeDtypeStruct((steps + 1, steps + 1), f32),
        ),
        in_specs=[vmem, vmem, vmem, smem],
        out_specs=(vmem, vmem, vmem),
        compiler_params=pltpu.CompilerParams(vmem_limit_bytes=4 * mebi),
        name="finish",
    )(parts, basis, x, shifts)
    return (sol.reshape(-1), res.reshape(-1), upper)


def solution(mesh):
    split = P(AXES)
    return jax.shard_map(
        body,
        mesh=mesh,
        in_specs=(P(AXES, None, None), P(AXES, None), split, split, split, P()),
        out_specs=(split, split, P()),
        check_vma=False,
    )
```

```python
import functools

import jax
import jax.numpy as jnp
from jax import lax
from jax.experimental import pallas as pl
from jax.experimental.pallas import tpu as pltpu
from jax.sharding import PartitionSpec as P

AXES = ("group", "slab")
WIDTH = 64
LANES = 128
REACH = 2
BANDS = 2 * REACH + 1
HALF = WIDTH // 2
ROWS = BANDS * HALF
CHUNK = 4
GROUP = 8


def between_chips(array):
    size = lax.axis_size(AXES)
    pairs = [(i, i + 1 if i % 2 else i - 1) for i in range(1, size - 1)]
    return lax.ppermute(array, AXES, pairs)


def within_chip(array):
    size = lax.axis_size(AXES)
    return lax.ppermute(array, AXES, [(i, i + 1 - 2 * (i % 2)) for i in range(size)])


def lane_ids(rows):
    return lax.broadcasted_iota(jnp.int32, (rows, LANES), 1)


def band_kernel(
    op_ref, adjacency_ref, valid_ref, start_ref, rhs_ref, outer_ref, inner_ref,
    held, adj_ref, counts_ref, in_sems, other_sems,
):
    elems, _, columns = op_ref.shape
    faces = columns // WIDTH - 1
    chunks = elems // CHUNK
    device = lax.axis_index(AXES)
    base = device * elems
    second = device % 2
    left = lane_ids(HALF) < WIDTH
    tail = GROUP * ROWS

    def origin(slot):
        half = slot // GROUP
        return slot - half * GROUP + GROUP * jnp.where(second == half, 0, 1)

    def arriving(chunk):
        source = op_ref.at[pl.ds(origin(chunk * CHUNK), CHUNK)]
        return pltpu.make_async_copy(source, held.at[pl.ds(chunk * CHUNK, CHUNK)], in_sems.at[chunk])

    for chunk in range(chunks):
        arriving(chunk).start()
    scalars = [
        pltpu.make_async_copy(adjacency_ref, adj_ref, other_sems.at[0]),
        pltpu.make_async_copy(valid_ref, counts_ref, other_sems.at[1]),
    ]
    extras = []
    for number, source in enumerate((start_ref, rhs_ref)):
        for place, target in enumerate((outer_ref, inner_ref)):
            rows = pl.ds(tail + 8 * number, 8)
            sem = other_sems.at[2 + 2 * number + place]
            extras.append(pltpu.make_async_copy(source, target.at[rows, :], sem))
    for copy in scalars + extras:
        copy.start()
    for copy in scalars:
        copy.wait()

    def one(slot, target, at):
        e = origin(slot)
        blocks = []
        for tile in range(columns // LANES):
            lanes = pl.ds(tile * LANES, LANES)
            top = held[slot, pl.ds(0, HALF), lanes]
            low = held[slot, pl.ds(HALF, HALF), lanes]
            blocks.append(jnp.where(left, top, pltpu.roll(low, WIDTH, 1)))
            blocks.append(jnp.where(left, pltpu.roll(top, WIDTH, 1), low))
        if columns % LANES:
            lanes = pl.ds(columns - WIDTH, WIDTH)
            top = held[slot, pl.ds(0, HALF), lanes]
            low = held[slot, pl.ds(HALF, HALF), lanes]
            blocks.append(jnp.concatenate([top, low], axis=1))
        count = counts_ref[e]
        place = []
        for face in range(faces):
            offset = adj_ref[face, e] - (base + e) + REACH
            place.append(jnp.where(face < count, offset, -1))
        for band in range(BANDS):
            rows = pl.ds(pl.multiple_of(at * ROWS + band * HALF, HALF), HALF)
            total = blocks[0] if band == REACH else None
            if band != REACH:
                for face in range(faces):
                    weight = jnp.where(place[face] == band, jnp.float32(1), jnp.float32(0))
                    term = blocks[face + 1] * weight
                    total = term if total is None else total + term
            target[rows, :] = total

    for half, target in enumerate((outer_ref, inner_ref)):

        def some(part, carry, half=half, target=target):
            chunk = half * (GROUP // CHUNK) + part
            arriving(chunk).wait()
            for k in range(CHUNK):
                at = part * CHUNK + k
                one(half * GROUP + at, target, at)
            return carry

        lax.fori_loop(0, GROUP // CHUNK, some, 0)
    for extra in extras:
        extra.wait()


def stacked_sums(terms, row):
    for span in (4, 2, 1):
        low = (row & span) == 0
        half = len(terms) // 2
        merged = []
        for a, b in zip(terms[:half], terms[half:]):
            kept = jnp.where(low, a, b)
            if span == 4:
                moved = pltpu.roll(jnp.where(low, b, a), 4, 0)
            else:
                moved = jnp.where(low, pltpu.roll(a, 8 - span, 0), pltpu.roll(b, span, 0))
            merged.append(kept + moved)
        terms = merged
    return terms[0]


def spread(ref, at, packed):
    left = lane_ids(8) < WIDTH
    turned = pltpu.roll(packed, WIDTH, 1)
    ref[pl.ds(at, 8, stride=2), :] = jnp.where(left, packed, turned)
    ref[pl.ds(at + 1, 8, stride=2), :] = jnp.where(left, turned, packed)


def times(ref, vecs, at):
    row = lax.broadcasted_iota(jnp.int32, (8, LANES), 0)
    half = lane_ids(HALF)
    left = half < WIDTH
    spot = half % WIDTH - lax.broadcasted_iota(jnp.int32, (HALF, LANES), 0)
    near = [vecs[pl.ds(at + (k - REACH), 1), :] for k in range(GROUP + 2 * REACH)]
    terms = []
    for k in range(GROUP):
        total = None
        for band in range(BANDS):
            rows = pl.ds(k * ROWS + band * HALF, HALF)
            term = ref[rows, :] * near[k + band]
            total = term if total is None else total + term
        top = jnp.sum(jnp.where(left, total, 0.0), axis=1, keepdims=True)
        low = jnp.sum(jnp.where(left, 0.0, total), axis=1, keepdims=True)
        placed = jnp.where(spot == 0, top, jnp.where(spot == HALF, low, 0.0))
        terms.append(jnp.sum(placed.reshape(HALF // 8, 8, LANES), axis=0))
    return stacked_sums(terms, row)


def applications(first, last, refs, vecs, level, shifts_ref):
    given = (last - first + 1) * level

    def apply(index, groups):
        at = pl.multiple_of((index - first) * level, 8)
        if first == 0:
            opening = index == 0
            source = pl.multiple_of(jnp.where(opening, given, at), 8)
            sign = jnp.where(opening, jnp.float32(-1), jnp.float32(1))
            scale = jnp.where(opening, jnp.float32(1), -shifts_ref[jnp.maximum(index - 1, 0)])
        else:
            source, sign, scale = at, None, -shifts_ref[index - 1]
        made = []
        for group in groups:
            place = GROUP * (group + 1)
            fresh = times(refs[group], vecs, at + place)
            if sign is not None:
                fresh = sign * fresh
            made.append((place, fresh + scale * vecs[pl.ds(source + place, 8), :]))
        for place, value in made:
            vecs[pl.ds(at + level + place, 8), :] = value

    def turn(index, carry):
        apply(index, range(4))
        return carry

    lax.fori_loop(first, last - 1, turn, 0)
    apply(last - 1, (1, 2))


def by_core(run, outer, own, inner):
    second = lax.axis_index(AXES) % 2 == 1

    @pl.when(second)
    def _():
        run(inner, own[::-1], outer)

    @pl.when(jnp.logical_not(second))
    def _():
        run(outer, own, inner)


def packed_rows(vecs, at):
    left = lane_ids(8) < WIDTH
    return jnp.where(left, vecs[pl.ds(at, 8, stride=2), :], vecs[pl.ds(at + 1, 8, stride=2), :])


def early_kernel(
    count, got_inner, own_inner, own_outer, got_outer, shifts_ref, basis_ref, last_ref, vecs
):
    level = 6 * GROUP

    def run(before, own, after):
        refs = (before, *own, after)
        tail = GROUP * ROWS
        for part, ref in enumerate((before, own[0], after)):
            spread(vecs, part * 2 * GROUP, ref[pl.ds(tail, 8), :])
            spread(vecs, (count + 1) * level + part * 2 * GROUP, ref[pl.ds(tail + 8, 8), :])
        applications(0, count, refs, vecs, level, shifts_ref)

    by_core(run, got_outer, (own_outer, own_inner), got_inner)
    for k in range(count):
        row = packed_rows(vecs, (k + 1) * level + 2 * GROUP)
        basis_ref[pl.ds(8 * k, 8), :] = row
        if k == count - 1:
            last_ref[...] = row


def late_kernel(
    count, size, vec_inner, vec_own, vec_outer, got_inner, own_inner, own_outer, got_outer,
    early_ref, shifts_ref, basis_ref, gram_ref, vecs,
):
    level = 6 * GROUP

    def run(before, own, after):
        refs = (before[1], *own, after[1])
        for part, ref in enumerate((before[0], vec_own, after[0])):
            spread(vecs, part * 2 * GROUP, ref[...])
        applications(count, size, refs, vecs, level, shifts_ref)

    by_core(run, (vec_outer, got_outer), (own_outer, own_inner), (vec_inner, got_inner))
    rows = [early_ref[pl.ds(8 * k, 8), :] for k in range(count)]
    for k in range(size - count):
        rows.append(packed_rows(vecs, (k + 1) * level + 2 * GROUP))
        basis_ref[pl.ds(8 * k, 8), :] = rows[-1]
    lane = lane_ids(8)
    total = jnp.zeros((8, LANES), jnp.float32)
    number = 0
    for i in range(size):
        for j in range(i, size):
            entry = jnp.sum(rows[i] * rows[j], axis=1, keepdims=True)
            total = jnp.where(lane == number, entry, total)
            number += 1
    gram = jnp.sum(total, axis=0, keepdims=True)
    gram_ref[...] = jnp.broadcast_to(gram, gram_ref.shape)


def partial_kernel(parts_ref, out_ref):
    total = jnp.sum(parts_ref[...], axis=0, keepdims=True)
    out_ref[...] = jnp.broadcast_to(total, out_ref.shape)


def inverse_root(value):
    guess = lax.rsqrt(value)
    return guess * (1.5 - 0.5 * value * guess * guess)


def finish_kernel(count, steps, parts_ref, early_ref, late_ref, start_ref, shifts_ref, sol_ref, res_ref, upper_ref):
    size = steps + 1
    lane = lane_ids(8)
    summed = jnp.broadcast_to(jnp.sum(parts_ref[...], axis=0, keepdims=True), (8, LANES))
    gram = {}
    number = 0
    for i in range(size):
        for j in range(i, size):
            entry = jnp.sum(jnp.where(lane == number, summed, 0.0), axis=1, keepdims=True)
            gram[i, j] = jnp.broadcast_to(entry, (8, LANES))
            number += 1
    factor = {}
    for k in range(size):
        turn = inverse_root(gram[k, k])
        for j in range(k, size):
            factor[k, j] = gram[k, j] * turn
        for i in range(k + 1, size):
            for j in range(i, size):
                gram[i, j] = gram[i, j] - factor[k, i] * factor[k, j]
    hess = {}
    for k in range(steps):
        for i in range(k + 1):
            hess[i, k] = factor[i, k] * shifts_ref[k] + factor[i, k + 1]
        hess[k + 1, k] = factor[k + 1, k + 1]
    target = [factor[0, 0]] + [jnp.zeros((8, LANES), jnp.float32)] * steps
    inverse = []
    for k in range(steps):
        a, b = hess[k, k], hess[k + 1, k]
        scale = inverse_root(a * a + b * b)
        cos, sin = a * scale, b * scale
        inverse.append(scale)
        for j in range(k + 1, steps):
            up, down = hess[k, j], hess[k + 1, j]
            hess[k, j] = cos * up + sin * down
            hess[k + 1, j] = cos * down - sin * up
        target[k], target[k + 1] = cos * target[k], -(sin * target[k])
    coeffs = [None] * steps
    for k in range(steps - 1, -1, -1):
        value = target[k]
        for j in range(k + 1, steps):
            value = value - hess[k, j] * coeffs[j]
        coeffs[k] = value * inverse[k]
    rows = []
    for ref in (early_ref, late_ref):
        rows += [ref[pl.ds(at, 8), :] for at in range(0, ref.shape[0], 8)]
    sol, res = 0.0, 0.0
    for k in range(steps):
        sol = sol + coeffs[k] * rows[k]
        res = res + coeffs[k] * (rows[k + 1] + shifts_ref[k] * rows[k])
    sol_ref[...] = start_ref[...] + sol
    res_ref[...] = rows[0] - res
    wide = lane_ids(16)
    tall = lax.broadcasted_iota(jnp.int32, (16, LANES), 0)
    scale = 1.0 / (count ** 0.5)
    upper = jnp.zeros((16, LANES), jnp.float32)
    for i in range(size):
        for j in range(i, size):
            entry = jnp.concatenate([factor[i, j]] * 2, axis=0) * scale
            upper = jnp.where((wide == j) & (tall == i), entry, upper)
    upper_ref[...] = upper[:size, :size]


def body(operator, adjacency, counts, rhs, start, shifts):
    elems, width, columns = operator.shape
    steps = shifts.shape[0]
    devices = lax.axis_size(AXES)
    slabs = lax.axis_size("slab")
    groups = lax.axis_size("group")
    packed = elems * width // LANES
    size = steps + 1
    early = size // 2
    block = GROUP * ROWS + 2 * packed
    level = 6 * GROUP
    vmem = pl.BlockSpec(memory_space=pltpu.VMEM)
    smem = pl.BlockSpec(memory_space=pltpu.SMEM)
    hbm = pl.BlockSpec(memory_space=pl.ANY)
    mebi = 1024 * 1024
    f32 = jnp.float32

    x = start.reshape(packed, LANES)
    b = rhs.reshape(packed, LANES)
    sources = (operator, adjacency.T, counts, x, b)
    own_outer, own_inner = pl.pallas_call(
        band_kernel,
        out_shape=(pltpu.VMEM((block, LANES), f32), pltpu.VMEM((block, LANES), f32)),
        in_specs=[hbm] * 5,
        out_specs=(vmem, vmem),
        scratch_shapes=[
            pltpu.VMEM(operator.shape, f32),
            pltpu.SMEM(adjacency.T.shape, jnp.int32),
            pltpu.SMEM(counts.shape, jnp.int32),
            pltpu.SemaphoreType.DMA((elems // CHUNK,)),
            pltpu.SemaphoreType.DMA((6,)),
        ],
        compiler_params=pltpu.CompilerParams(vmem_limit_bytes=16 * mebi),
        name="bands",
    )(*(pltpu.with_memory_space_constraint(source, pltpu.HBM) for source in sources))
    bands = (within_chip(own_inner), own_inner, own_outer, between_chips(own_outer))
    first, last = pl.pallas_call(
        functools.partial(early_kernel, early),
        out_shape=(
            jax.ShapeDtypeStruct((8 * early, LANES), f32),
            jax.ShapeDtypeStruct((packed, LANES), f32),
        ),
        in_specs=[vmem] * 4 + [smem],
        out_specs=(vmem, vmem),
        scratch_shapes=[pltpu.VMEM(((early + 2) * level, LANES), f32)],
        compiler_params=pltpu.CompilerParams(vmem_limit_bytes=16 * mebi),
        name="early",
    )(*bands, shifts)
    rest, gram = pl.pallas_call(
        functools.partial(late_kernel, early, size),
        out_shape=(
            jax.ShapeDtypeStruct((8 * (size - early), LANES), f32),
            jax.ShapeDtypeStruct((slabs, LANES), f32),
        ),
        in_specs=[vmem] * 8 + [smem],
        out_specs=(vmem, vmem),
        scratch_shapes=[pltpu.VMEM(((size - early + 1) * level, LANES), f32)],
        compiler_params=pltpu.CompilerParams(vmem_limit_bytes=16 * mebi),
        name="late",
    )(within_chip(last), last, between_chips(last), *bands, first, shifts)
    parts = lax.all_to_all(gram, "slab", 0, 0, tiled=True)
    parts = pl.pallas_call(
        partial_kernel,
        out_shape=jax.ShapeDtypeStruct((groups, LANES), f32),
        in_specs=[vmem],
        out_specs=vmem,
        compiler_params=pltpu.CompilerParams(vmem_limit_bytes=4 * mebi),
        name="partial",
    )(parts)
    parts = lax.all_to_all(parts, "group", 0, 0, tiled=True)
    sol, res, upper = pl.pallas_call(
        functools.partial(finish_kernel, devices * elems * width, steps),
        out_shape=(
            jax.ShapeDtypeStruct((packed, LANES), f32),
            jax.ShapeDtypeStruct((packed, LANES), f32),
            jax.ShapeDtypeStruct((steps + 1, steps + 1), f32),
        ),
        in_specs=[vmem, vmem, vmem, vmem, smem],
        out_specs=(vmem, vmem, vmem),
        compiler_params=pltpu.CompilerParams(vmem_limit_bytes=4 * mebi),
        name="finish",
    )(parts, first, rest, x, shifts)
    return (sol.reshape(-1), res.reshape(-1), upper)


def solution(mesh):
    split = P(AXES)
    return jax.shard_map(
        body,
        mesh=mesh,
        in_specs=(P(AXES, None, None), P(AXES, None), split, split, split, P()),
        out_specs=(split, split, P()),
        check_vma=False,
    )
```

```python
import functools

import jax
import jax.numpy as jnp
from jax import lax
from jax.experimental import pallas as pl
from jax.experimental.pallas import tpu as pltpu
from jax.sharding import PartitionSpec as P

AXES = ("group", "slab")
WIDTH = 64
LANES = 128
REACH = 2
BANDS = 2 * REACH + 1
HALF = WIDTH // 2
ROWS = BANDS * HALF
CHUNK = 4
PAD = 8
GROUP = 8


def between_chips(array):
    size = lax.axis_size(AXES)
    pairs = [(i, i + 1 if i % 2 else i - 1) for i in range(1, size - 1)]
    return lax.ppermute(array, AXES, pairs)


def within_chip(array):
    size = lax.axis_size(AXES)
    return lax.ppermute(array, AXES, [(i, i + 1 - 2 * (i % 2)) for i in range(size)])


def across(array, toward):
    size = lax.axis_size(AXES)
    pairs = [(i, i + toward * (4 * (i % 2) - 2)) for i in range(size)]
    return lax.ppermute(array, AXES, [(i, j) for i, j in pairs if 0 <= j < size])


def lane_ids(rows):
    return lax.broadcasted_iota(jnp.int32, (rows, LANES), 1)


def band_kernel(
    op_ref, adjacency_ref, valid_ref, start_ref, rhs_ref, outer_ref, inner_ref,
    held, adj_ref, counts_ref, in_sems, other_sems,
):
    elems, _, columns = op_ref.shape
    faces = columns // WIDTH - 1
    chunks = elems // CHUNK
    device = lax.axis_index(AXES)
    base = device * elems
    second = device % 2
    left = lane_ids(HALF) < WIDTH
    tail = GROUP * ROWS

    def origin(slot):
        half = slot // GROUP
        return slot - half * GROUP + GROUP * jnp.where(second == half, 0, 1)

    def arriving(chunk):
        source = op_ref.at[pl.ds(origin(chunk * CHUNK), CHUNK)]
        return pltpu.make_async_copy(source, held.at[pl.ds(chunk * CHUNK, CHUNK)], in_sems.at[chunk])

    for chunk in range(chunks):
        arriving(chunk).start()
    scalars = [
        pltpu.make_async_copy(adjacency_ref, adj_ref, other_sems.at[0]),
        pltpu.make_async_copy(valid_ref, counts_ref, other_sems.at[1]),
    ]
    extras = []
    for number, source in enumerate((start_ref, rhs_ref)):
        for place, target in enumerate((outer_ref, inner_ref)):
            rows = pl.ds(tail + 8 * number, 8)
            sem = other_sems.at[2 + 2 * number + place]
            extras.append(pltpu.make_async_copy(source, target.at[rows, :], sem))
    for copy in scalars + extras:
        copy.start()
    for copy in scalars:
        copy.wait()

    def one(slot, target, at):
        e = origin(slot)
        blocks = []
        for tile in range(columns // LANES):
            lanes = pl.ds(tile * LANES, LANES)
            top = held[slot, pl.ds(0, HALF), lanes]
            low = held[slot, pl.ds(HALF, HALF), lanes]
            blocks.append(jnp.where(left, top, pltpu.roll(low, WIDTH, 1)))
            blocks.append(jnp.where(left, pltpu.roll(top, WIDTH, 1), low))
        if columns % LANES:
            lanes = pl.ds(columns - WIDTH, WIDTH)
            top = held[slot, pl.ds(0, HALF), lanes]
            low = held[slot, pl.ds(HALF, HALF), lanes]
            blocks.append(jnp.concatenate([top, low], axis=1))
        count = counts_ref[e]
        place = []
        for face in range(faces):
            offset = adj_ref[face, e] - (base + e) + REACH
            place.append(jnp.where(face < count, offset, -1))
        for band in range(BANDS):
            rows = pl.ds(pl.multiple_of(at * ROWS + band * HALF, HALF), HALF)
            total = blocks[0] if band == REACH else None
            if band != REACH:
                for face in range(faces):
                    weight = jnp.where(place[face] == band, jnp.float32(1), jnp.float32(0))
                    term = blocks[face + 1] * weight
                    total = term if total is None else total + term
            target[rows, :] = total

    for half, target in enumerate((outer_ref, inner_ref)):

        def some(part, carry, half=half, target=target):
            chunk = half * (GROUP // CHUNK) + part
            arriving(chunk).wait()
            for k in range(CHUNK):
                at = part * CHUNK + k
                one(half * GROUP + at, target, at)
            return carry

        lax.fori_loop(0, GROUP // CHUNK, some, 0)
    for extra in extras:
        extra.wait()


LEVEL = 6 * GROUP + 2 * PAD


def stacked_sums(terms, row):
    for span in (4, 2, 1):
        low = (row & span) == 0
        half = len(terms) // 2
        merged = []
        for a, b in zip(terms[:half], terms[half:]):
            kept = jnp.where(low, a, b)
            if span == 4:
                moved = pltpu.roll(jnp.where(low, b, a), 4, 0)
            else:
                moved = jnp.where(low, pltpu.roll(a, 8 - span, 0), pltpu.roll(b, span, 0))
            merged.append(kept + moved)
        terms = merged
    return terms[0]


def spread(ref, at, packed):
    left = lane_ids(8) < WIDTH
    turned = pltpu.roll(packed, WIDTH, 1)
    ref[pl.ds(at, 8, stride=2), :] = jnp.where(left, packed, turned)
    ref[pl.ds(at + 1, 8, stride=2), :] = jnp.where(left, turned, packed)


def times(ref, vecs, at):
    row = lax.broadcasted_iota(jnp.int32, (8, LANES), 0)
    half = lane_ids(HALF)
    left = half < WIDTH
    spot = half % WIDTH - lax.broadcasted_iota(jnp.int32, (HALF, LANES), 0)
    near = [vecs[pl.ds(at + (k - REACH), 1), :] for k in range(GROUP + 2 * REACH)]
    terms = []
    for k in range(GROUP):
        total = None
        for band in range(BANDS):
            rows = pl.ds(k * ROWS + band * HALF, HALF)
            term = ref[rows, :] * near[k + band]
            total = term if total is None else total + term
        top = jnp.sum(jnp.where(left, total, 0.0), axis=1, keepdims=True)
        low = jnp.sum(jnp.where(left, 0.0, total), axis=1, keepdims=True)
        placed = jnp.where(spot == 0, top, jnp.where(spot == HALF, low, 0.0))
        terms.append(jnp.sum(placed.reshape(HALF // 8, 8, LANES), axis=0))
    return stacked_sums(terms, row)


def application(index, groups, refs, vecs, shifts_ref):
    levels = vecs.shape[0] // LEVEL
    at = pl.multiple_of(index * LEVEL, 8)
    opening = index == 0
    source = pl.multiple_of(jnp.where(opening, (levels - 1) * LEVEL, at), 8)
    sign = jnp.where(opening, jnp.float32(-1), jnp.float32(1))
    scale = jnp.where(opening, jnp.float32(1), -shifts_ref[jnp.maximum(index - 1, 0)])
    made = []
    for group in groups:
        place = PAD + GROUP * group
        fresh = times(refs[group], vecs, at + place)
        made.append((place, sign * fresh + scale * vecs[pl.ds(source + place, 8), :]))
    for place, value in made:
        vecs[pl.ds(at + LEVEL + place, 8), :] = value


def applications(plan, refs, vecs, shifts_ref):
    for first, last, groups in plan:

        def turn(index, carry, groups=groups):
            application(index, groups, refs, vecs, shifts_ref)
            return carry

        if last - first == 1:
            turn(jnp.int32(first), 0)
        else:
            lax.fori_loop(first, last, turn, 0)


def by_core(run):
    second = lax.axis_index(AXES) % 2 == 1

    @pl.when(second)
    def _():
        run(lambda items: items[::-1], True)

    @pl.when(jnp.logical_not(second))
    def _():
        run(lambda items: items, False)


def fill_far(vecs, row, at):
    packed = jnp.broadcast_to(row, (8, LANES))
    turned = pltpu.roll(packed, WIDTH, 1)
    left = lane_ids(8) < WIDTH
    vecs[pl.ds(at, 1), :] = jnp.where(left, packed, turned)[:1]
    vecs[pl.ds(at + 1, 1), :] = jnp.where(left, turned, packed)[:1]


def early_kernel(
    plan, other_far, other_near, own_inner, own_outer, near_ref, shifts_ref, vecs
):
    empty = jnp.zeros((8, LANES), jnp.float32)
    for at in range(0, vecs.shape[0], 8):
        vecs[pl.ds(at, 8), :] = empty

    def run(order, turned):
        refs = order([None, near_ref, own_outer, own_inner, other_near, other_far])
        tail = GROUP * ROWS
        given = vecs.shape[0] - LEVEL
        for part, ref in enumerate(order([near_ref, own_outer, other_near])):
            at = PAD + part * 2 * GROUP
            spread(vecs, at, ref[pl.ds(tail, 8), :])
            spread(vecs, given + at, ref[pl.ds(tail + 8, 8), :])
        applications([(i, j, order_groups(groups, turned)) for i, j, groups in plan], refs, vecs, shifts_ref)

    by_core(run)


def order_groups(groups, turned):
    return [5 - group for group in groups] if turned else groups


def late_kernel(
    plan, size, far_outer, far_inner, other_far, other_near, own_inner, own_outer, near_ref, rim_ref,
    early_ref, shifts_ref, basis_ref, gram_ref, vecs,
):
    for at in range(0, vecs.shape[0], 8):
        vecs[pl.ds(at, 8), :] = early_ref[pl.ds(at, 8), :]

    def run(order, turned):
        refs = order([rim_ref, near_ref, own_outer, own_inner, other_near, other_far])
        before, after = order([far_outer, far_inner])
        fill_far(vecs, before[pl.ds(7, 1), :], PAD - 2)
        fill_far(vecs, after[pl.ds(0, 1), :], PAD + 6 * GROUP)
        applications([(i, j, order_groups(groups, turned)) for i, j, groups in plan], refs, vecs, shifts_ref)

    by_core(run)
    left = lane_ids(8) < WIDTH
    rows = []
    for k in range(size):
        at = (k + 1) * LEVEL + PAD + 2 * GROUP
        even, odd = vecs[pl.ds(at, 8, stride=2), :], vecs[pl.ds(at + 1, 8, stride=2), :]
        rows.append(jnp.where(left, even, odd))
        basis_ref[pl.ds(8 * k, 8), :] = rows[-1]
    lane = lane_ids(8)
    total = jnp.zeros((8, LANES), jnp.float32)
    number = 0
    for i in range(size):
        for j in range(i, size):
            entry = jnp.sum(rows[i] * rows[j], axis=1, keepdims=True)
            total = jnp.where(lane == number, entry, total)
            number += 1
    gram = jnp.sum(total, axis=0, keepdims=True)
    gram_ref[...] = jnp.broadcast_to(gram, gram_ref.shape)


def plans(size):
    early, late = [], []
    for k in range(size):
        low, high = REACH * k - 2 * GROUP, 4 * GROUP - 1 - REACH * k
        ranges = [[(low + GROUP, high - REACH)], [(low, low + GROUP - 1), (high - REACH + 1, high)]]
        for plan, wanted in zip((early, late), ranges):
            groups = [
                g
                for g in range(6)
                if any(8 * g - 9 >= start and 8 * g - 16 <= end for start, end in wanted)
            ]
            if plan and plan[-1][2] == groups:
                plan[-1] = (plan[-1][0], k + 1, groups)
            else:
                plan.append((k, k + 1, groups))
    return early, late


def partial_kernel(parts_ref, out_ref):
    total = jnp.sum(parts_ref[...], axis=0, keepdims=True)
    out_ref[...] = jnp.broadcast_to(total, out_ref.shape)


def inverse_root(value):
    guess = lax.rsqrt(value)
    return guess * (1.5 - 0.5 * value * guess * guess)


def finish_kernel(count, steps, parts_ref, basis_ref, start_ref, shifts_ref, sol_ref, res_ref, upper_ref):
    size = steps + 1
    lane = lane_ids(8)
    summed = jnp.broadcast_to(jnp.sum(parts_ref[...], axis=0, keepdims=True), (8, LANES))
    gram = {}
    number = 0
    for i in range(size):
        for j in range(i, size):
            entry = jnp.sum(jnp.where(lane == number, summed, 0.0), axis=1, keepdims=True)
            gram[i, j] = jnp.broadcast_to(entry, (8, LANES))
            number += 1
    factor = {}
    for k in range(size):
        turn = inverse_root(gram[k, k])
        for j in range(k, size):
            factor[k, j] = gram[k, j] * turn
        for i in range(k + 1, size):
            for j in range(i, size):
                gram[i, j] = gram[i, j] - factor[k, i] * factor[k, j]
    hess = {}
    for k in range(steps):
        for i in range(k + 1):
            hess[i, k] = factor[i, k] * shifts_ref[k] + factor[i, k + 1]
        hess[k + 1, k] = factor[k + 1, k + 1]
    target = [factor[0, 0]] + [jnp.zeros((8, LANES), jnp.float32)] * steps
    inverse = []
    for k in range(steps):
        a, b = hess[k, k], hess[k + 1, k]
        scale = inverse_root(a * a + b * b)
        cos, sin = a * scale, b * scale
        inverse.append(scale)
        for j in range(k + 1, steps):
            up, down = hess[k, j], hess[k + 1, j]
            hess[k, j] = cos * up + sin * down
            hess[k + 1, j] = cos * down - sin * up
        target[k], target[k + 1] = cos * target[k], -(sin * target[k])
    coeffs = [None] * steps
    for k in range(steps - 1, -1, -1):
        value = target[k]
        for j in range(k + 1, steps):
            value = value - hess[k, j] * coeffs[j]
        coeffs[k] = value * inverse[k]
    rows = [basis_ref[pl.ds(8 * k, 8), :] for k in range(size)]
    sol, res = 0.0, 0.0
    for k in range(steps):
        sol = sol + coeffs[k] * rows[k]
        res = res + coeffs[k] * (rows[k + 1] + shifts_ref[k] * rows[k])
    sol_ref[...] = start_ref[...] + sol
    res_ref[...] = rows[0] - res
    wide = lane_ids(16)
    tall = lax.broadcasted_iota(jnp.int32, (16, LANES), 0)
    scale = 1.0 / (count ** 0.5)
    upper = jnp.zeros((16, LANES), jnp.float32)
    for i in range(size):
        for j in range(i, size):
            entry = jnp.concatenate([factor[i, j]] * 2, axis=0) * scale
            upper = jnp.where((wide == j) & (tall == i), entry, upper)
    upper_ref[...] = upper[:size, :size]


def body(operator, adjacency, counts, rhs, start, shifts):
    elems, width, columns = operator.shape
    steps = shifts.shape[0]
    devices = lax.axis_size(AXES)
    slabs = lax.axis_size("slab")
    groups = lax.axis_size("group")
    packed = elems * width // LANES
    size = steps + 1
    early, late = plans(size)
    block = GROUP * ROWS + 2 * packed
    rows = (size + 2) * LEVEL
    vmem = pl.BlockSpec(memory_space=pltpu.VMEM)
    smem = pl.BlockSpec(memory_space=pltpu.SMEM)
    hbm = pl.BlockSpec(memory_space=pl.ANY)
    mebi = 1024 * 1024
    f32 = jnp.float32

    x = start.reshape(packed, LANES)
    b = rhs.reshape(packed, LANES)
    sources = (operator, adjacency.T, counts, x, b)
    own_outer, own_inner = pl.pallas_call(
        band_kernel,
        out_shape=(pltpu.VMEM((block, LANES), f32), pltpu.VMEM((block, LANES), f32)),
        in_specs=[hbm] * 5,
        out_specs=(vmem, vmem),
        scratch_shapes=[
            pltpu.VMEM(operator.shape, f32),
            pltpu.SMEM(adjacency.T.shape, jnp.int32),
            pltpu.SMEM(counts.shape, jnp.int32),
            pltpu.SemaphoreType.DMA((elems // CHUNK,)),
            pltpu.SemaphoreType.DMA((6,)),
        ],
        compiler_params=pltpu.CompilerParams(vmem_limit_bytes=16 * mebi),
        name="bands",
    )(*(pltpu.with_memory_space_constraint(source, pltpu.HBM) for source in sources))
    other_far = within_chip(own_outer)
    other_near = within_chip(own_inner)
    rim = between_chips(own_inner)
    near = between_chips(own_outer)
    held = pl.pallas_call(
        functools.partial(early_kernel, early),
        out_shape=jax.ShapeDtypeStruct((rows, LANES), f32),
        in_specs=[vmem] * 5 + [smem],
        out_specs=vmem,
        compiler_params=pltpu.CompilerParams(vmem_limit_bytes=16 * mebi),
        name="early",
    )(other_far, other_near, own_inner, own_outer, near, shifts)
    basis, gram = pl.pallas_call(
        functools.partial(late_kernel, late, size),
        out_shape=(
            jax.ShapeDtypeStruct((8 * size, LANES), f32),
            jax.ShapeDtypeStruct((slabs, LANES), f32),
        ),
        in_specs=[vmem] * 9 + [smem],
        out_specs=(vmem, vmem),
        scratch_shapes=[pltpu.VMEM((rows, LANES), f32)],
        compiler_params=pltpu.CompilerParams(vmem_limit_bytes=16 * mebi),
        name="late",
    )(
        across(x, -1), across(x, 1), other_far, other_near, own_inner, own_outer, near, rim,
        held, shifts,
    )
    parts = lax.all_to_all(gram, "slab", 0, 0, tiled=True)
    parts = pl.pallas_call(
        partial_kernel,
        out_shape=jax.ShapeDtypeStruct((groups, LANES), f32),
        in_specs=[vmem],
        out_specs=vmem,
        compiler_params=pltpu.CompilerParams(vmem_limit_bytes=4 * mebi),
        name="partial",
    )(parts)
    parts = lax.all_to_all(parts, "group", 0, 0, tiled=True)
    sol, res, upper = pl.pallas_call(
        functools.partial(finish_kernel, devices * elems * width, steps),
        out_shape=(
            jax.ShapeDtypeStruct((packed, LANES), f32),
            jax.ShapeDtypeStruct((packed, LANES), f32),
            jax.ShapeDtypeStruct((steps + 1, steps + 1), f32),
        ),
        in_specs=[vmem, vmem, vmem, smem],
        out_specs=(vmem, vmem, vmem),
        compiler_params=pltpu.CompilerParams(vmem_limit_bytes=4 * mebi),
        name="finish",
    )(parts, basis, x, shifts)
    return (sol.reshape(-1), res.reshape(-1), upper)


def solution(mesh):
    split = P(AXES)
    return jax.shard_map(
        body,
        mesh=mesh,
        in_specs=(P(AXES, None, None), P(AXES, None), split, split, split, P()),
        out_specs=(split, split, P()),
        check_vma=False,
    )
```

```python
import functools

import jax
import jax.numpy as jnp
from jax import lax
from jax.experimental import pallas as pl
from jax.experimental.pallas import tpu as pltpu
from jax.sharding import PartitionSpec as P

AXES = ("group", "slab")
WIDTH = 64
LANES = 128
REACH = 2
BANDS = 2 * REACH + 1
HALF = WIDTH // 2
ROWS = BANDS * HALF
CHUNK = 4
GROUP = 8
RIM = 2
BODY = 10
INNER = 12
PAD = 4
LEVEL = 56


def between_chips(array):
    size = lax.axis_size(AXES)
    pairs = [(i, i + 1 if i % 2 else i - 1) for i in range(1, size - 1)]
    return lax.ppermute(array, AXES, pairs)


def within_chip(array):
    size = lax.axis_size(AXES)
    return lax.ppermute(array, AXES, [(i, i + 1 - 2 * (i % 2)) for i in range(size)])


def lane_ids(rows):
    return lax.broadcasted_iota(jnp.int32, (rows, LANES), 1)


def band_kernel(
    op_ref, adjacency_ref, valid_ref, start_ref, rhs_ref, rim_ref, body_ref, inner_ref,
    held, adj_ref, counts_ref, in_sems, other_sems,
):
    elems, _, columns = op_ref.shape
    faces = columns // WIDTH - 1
    chunks = elems // CHUNK
    device = lax.axis_index(AXES)
    base = device * elems
    second = device % 2
    left = lane_ids(HALF) < WIDTH

    def origin(chunk):
        return jnp.where(second == 1, elems - CHUNK * (chunk + 1), CHUNK * chunk)

    def arriving(chunk):
        part = pl.ds(origin(chunk), CHUNK)
        return pltpu.make_async_copy(op_ref.at[part], held.at[part], in_sems.at[chunk])

    for chunk in range(chunks):
        arriving(chunk).start()
    scalars = [
        pltpu.make_async_copy(adjacency_ref, adj_ref, other_sems.at[0]),
        pltpu.make_async_copy(valid_ref, counts_ref, other_sems.at[1]),
    ]
    extras = []
    for number, source in enumerate((start_ref, rhs_ref)):
        for place, (target, size) in enumerate(((rim_ref, RIM), (inner_ref, INNER))):
            rows = pl.ds(size * ROWS + 8 * number, 8)
            sem = other_sems.at[2 + 2 * number + place]
            extras.append(pltpu.make_async_copy(source, target.at[rows, :], sem))
    for copy in scalars + extras:
        copy.start()
    for copy in scalars:
        copy.wait()

    def one(e, targets):
        blocks = []
        for tile in range(columns // LANES):
            lanes = pl.ds(tile * LANES, LANES)
            top = held[e, pl.ds(0, HALF), lanes]
            low = held[e, pl.ds(HALF, HALF), lanes]
            blocks.append(jnp.where(left, top, pltpu.roll(low, WIDTH, 1)))
            blocks.append(jnp.where(left, pltpu.roll(top, WIDTH, 1), low))
        if columns % LANES:
            lanes = pl.ds(columns - WIDTH, WIDTH)
            top = held[e, pl.ds(0, HALF), lanes]
            low = held[e, pl.ds(HALF, HALF), lanes]
            blocks.append(jnp.concatenate([top, low], axis=1))
        count = counts_ref[e]
        place = []
        for face in range(faces):
            offset = adj_ref[face, e] - (base + e) + REACH
            place.append(jnp.where(face < count, offset, -1))
        for band in range(BANDS):
            total = blocks[0] if band == REACH else None
            if band != REACH:
                for face in range(faces):
                    weight = jnp.where(place[face] == band, jnp.float32(1), jnp.float32(0))
                    term = blocks[face + 1] * weight
                    total = term if total is None else total + term
            for target, at in targets:
                target[pl.ds(pl.multiple_of(at * ROWS + band * HALF, HALF), HALF), :] = total

    in_body = jnp.where(second == 1, elems - RIM - BODY, RIM)
    in_inner = jnp.where(second == 1, 0, elems - INNER)
    arriving(0).wait()
    for k in range(RIM):
        e = jnp.where(second == 1, elems - RIM, 0) + k
        one(e, [(rim_ref, k)])
    for k in range(CHUNK - RIM):
        e = jnp.where(second == 1, elems - CHUNK, RIM) + k
        one(e, [(body_ref, e - in_body)])

    def some(chunk, carry):
        arriving(chunk).wait()
        for k in range(CHUNK):
            e = origin(chunk) + k
            one(e, [(body_ref, e - in_body), (inner_ref, e - in_inner)])
        return carry

    lax.fori_loop(1, chunks - 1, some, 0)
    arriving(chunks - 1).wait()
    for k in range(CHUNK):
        e = origin(chunks - 1) + k
        one(e, [(inner_ref, e - in_inner)])
    for extra in extras:
        extra.wait()


def stacked_sums(terms, row):
    for span in (4, 2, 1):
        low = (row & span) == 0
        half = len(terms) // 2
        merged = []
        for a, b in zip(terms[:half], terms[half:]):
            kept = jnp.where(low, a, b)
            if span == 4:
                moved = pltpu.roll(jnp.where(low, b, a), 4, 0)
            else:
                moved = jnp.where(low, pltpu.roll(a, 8 - span, 0), pltpu.roll(b, span, 0))
            merged.append(kept + moved)
        terms = merged
    return terms[0]


def spread(ref, at, packed):
    left = lane_ids(8) < WIDTH
    turned = pltpu.roll(packed, WIDTH, 1)
    ref[pl.ds(at, 8, stride=2), :] = jnp.where(left, packed, turned)
    ref[pl.ds(at + 1, 8, stride=2), :] = jnp.where(left, turned, packed)


def times(find, place, vecs, at):
    row = lax.broadcasted_iota(jnp.int32, (8, LANES), 0)
    half = lane_ids(HALF)
    left = half < WIDTH
    spot = half % WIDTH - lax.broadcasted_iota(jnp.int32, (HALF, LANES), 0)
    near = [vecs[pl.ds(at + (k - REACH), 1), :] for k in range(GROUP + 2 * REACH)]
    terms = []
    for k in range(GROUP):
        ref, spare = find(place + k)
        total = None
        for band in range(BANDS):
            rows = pl.ds(spare * ROWS + band * HALF, HALF)
            term = ref[rows, :] * near[k + band]
            total = term if total is None else total + term
        top = jnp.sum(jnp.where(left, total, 0.0), axis=1, keepdims=True)
        low = jnp.sum(jnp.where(left, 0.0, total), axis=1, keepdims=True)
        placed = jnp.where(spot == 0, top, jnp.where(spot == HALF, low, 0.0))
        terms.append(jnp.sum(placed.reshape(HALF // 8, 8, LANES), axis=0))
    return stacked_sums(terms, row)


def row_of(place):
    return PAD + 2 * GROUP + place


def application(at, find, places, vecs, combine):
    made = []
    for place in places:
        fresh = times(find, place, vecs, at + row_of(place))
        made.append((row_of(place), combine(fresh, row_of(place))))
    for row, value in made:
        vecs[pl.ds(at + LEVEL + row, 8), :] = value


def by_core(run):
    second = lax.axis_index(AXES) % 2 == 1
    pl.when(second)(lambda: run(True))
    pl.when(jnp.logical_not(second))(lambda: run(False))


def finder(turned, rim, body, inner, far_rim, far_body, far_inner):
    def find(place):
        out = 15 - place if turned else place
        if out < -RIM:
            ref, first, size = far_body, -RIM - BODY, BODY
        elif out < 0:
            ref, first, size = far_rim, -RIM, RIM
        elif out < RIM:
            ref, first, size = rim, 0, RIM
        elif out < 16 - INNER:
            ref, first, size = body, RIM, BODY
        elif out < 16:
            ref, first, size = inner, 16 - INNER, INNER
        else:
            ref, first, size = far_inner, 16, INNER
        spare = out - first
        assert 0 <= spare < size
        return ref, size - 1 - spare if turned else spare

    return find


def packed_rows(vecs, level):
    left = lane_ids(8) < WIDTH
    at = level * LEVEL + row_of(0)
    return jnp.where(left, vecs[pl.ds(at, 8, stride=2), :], vecs[pl.ds(at + 1, 8, stride=2), :])


def early_kernel(rim, body, inner, far_rim, far_inner, shifts_ref, basis_ref, last_ref, vecs):
    def run(turned):
        find = finder(turned, rim, body, inner, far_rim, None, far_inner)
        tails = [(far_rim, RIM), (rim, RIM), (far_inner, INNER)]
        for part, (ref, size) in enumerate(tails[::-1] if turned else tails):
            at = PAD + part * 2 * GROUP
            spread(vecs, at, ref[pl.ds(size * ROWS, 8), :])
            spread(vecs, 3 * LEVEL + at, ref[pl.ds(size * ROWS + 8, 8), :])
        places = [GROUP * k + (-6 if turned else -2) for k in range(3)]
        application(
            0, find, places, vecs, lambda fresh, row: vecs[pl.ds(3 * LEVEL + row, 8), :] - fresh
        )
        shift = shifts_ref[0]
        application(
            LEVEL, find, (0, GROUP), vecs, lambda fresh, row: fresh - shift * vecs[pl.ds(LEVEL + row, 8), :]
        )

    by_core(run)
    basis_ref[pl.ds(0, 8), :] = packed_rows(vecs, 1)
    last = packed_rows(vecs, 2)
    basis_ref[pl.ds(8, 8), :] = last
    last_ref[...] = last


def late_kernel(
    size, vec_inner, vec_outer, rim, body, inner, far_rim, far_inner, far_body,
    early_ref, shifts_ref, basis_ref, gram_ref, vecs,
):
    known = early_ref.shape[0] // 8

    def run(turned):
        find = finder(turned, rim, body, inner, far_rim, far_body, far_inner)
        vectors = [vec_outer[...], early_ref[pl.ds(8 * known - 8, 8), :], vec_inner[...]]
        for part, vector in enumerate(vectors[::-1] if turned else vectors):
            spread(vecs, PAD + part * 2 * GROUP, vector)

        def turn(index, carry, places):
            at = pl.multiple_of((index - known) * LEVEL, 8)
            shift = shifts_ref[index - 1]
            application(
                at, find, places, vecs, lambda fresh, row: fresh - shift * vecs[pl.ds(at + row, 8), :]
            )
            return carry

        wide = [GROUP * k - RIM - BODY for k in range(5)]
        narrow = wide[1:4]
        split = next(k for k in range(known, size) if REACH * (size - 1 - k) <= -narrow[0])
        lax.fori_loop(known, split, functools.partial(turn, places=wide), 0)
        lax.fori_loop(split, size, functools.partial(turn, places=narrow), 0)

    by_core(run)
    rows = [early_ref[pl.ds(8 * k, 8), :] for k in range(known)]
    rows += [packed_rows(vecs, k - known + 1) for k in range(known, size)]
    for k in range(size):
        basis_ref[pl.ds(8 * k, 8), :] = rows[k]
    lane = lane_ids(8)
    total = jnp.zeros((8, LANES), jnp.float32)
    number = 0
    for i in range(size):
        for j in range(i, size):
            entry = jnp.sum(rows[i] * rows[j], axis=1, keepdims=True)
            total = jnp.where(lane == number, entry, total)
            number += 1
    gram = jnp.sum(total, axis=0, keepdims=True)
    gram_ref[...] = jnp.broadcast_to(gram, gram_ref.shape)


def partial_kernel(parts_ref, out_ref):
    total = jnp.sum(parts_ref[...], axis=0, keepdims=True)
    out_ref[...] = jnp.broadcast_to(total, out_ref.shape)


def inverse_root(value):
    guess = lax.rsqrt(value)
    return guess * (1.5 - 0.5 * value * guess * guess)


def finish_kernel(count, steps, parts_ref, basis_ref, start_ref, shifts_ref, sol_ref, res_ref, upper_ref):
    size = steps + 1
    lane = lane_ids(8)
    summed = jnp.broadcast_to(jnp.sum(parts_ref[...], axis=0, keepdims=True), (8, LANES))
    gram = {}
    number = 0
    for i in range(size):
        for j in range(i, size):
            entry = jnp.sum(jnp.where(lane == number, summed, 0.0), axis=1, keepdims=True)
            gram[i, j] = jnp.broadcast_to(entry, (8, LANES))
            number += 1
    factor = {}
    for k in range(size):
        turn = inverse_root(gram[k, k])
        for j in range(k, size):
            factor[k, j] = gram[k, j] * turn
        for i in range(k + 1, size):
            for j in range(i, size):
                gram[i, j] = gram[i, j] - factor[k, i] * factor[k, j]
    hess = {}
    for k in range(steps):
        for i in range(k + 1):
            hess[i, k] = factor[i, k] * shifts_ref[k] + factor[i, k + 1]
        hess[k + 1, k] = factor[k + 1, k + 1]
    target = [factor[0, 0]] + [jnp.zeros((8, LANES), jnp.float32)] * steps
    inverse = []
    for k in range(steps):
        a, b = hess[k, k], hess[k + 1, k]
        scale = inverse_root(a * a + b * b)
        cos, sin = a * scale, b * scale
        inverse.append(scale)
        for j in range(k + 1, steps):
            up, down = hess[k, j], hess[k + 1, j]
            hess[k, j] = cos * up + sin * down
            hess[k + 1, j] = cos * down - sin * up
        target[k], target[k + 1] = cos * target[k], -(sin * target[k])
    coeffs = [None] * steps
    for k in range(steps - 1, -1, -1):
        value = target[k]
        for j in range(k + 1, steps):
            value = value - hess[k, j] * coeffs[j]
        coeffs[k] = value * inverse[k]
    rows = [basis_ref[pl.ds(8 * k, 8), :] for k in range(size)]
    sol, res = 0.0, 0.0
    for k in range(steps):
        sol = sol + coeffs[k] * rows[k]
        res = res + coeffs[k] * (rows[k + 1] + shifts_ref[k] * rows[k])
    sol_ref[...] = start_ref[...] + sol
    res_ref[...] = rows[0] - res
    wide = lane_ids(16)
    tall = lax.broadcasted_iota(jnp.int32, (16, LANES), 0)
    scale = 1.0 / (count ** 0.5)
    upper = jnp.zeros((16, LANES), jnp.float32)
    for i in range(size):
        for j in range(i, size):
            entry = jnp.concatenate([factor[i, j]] * 2, axis=0) * scale
            upper = jnp.where((wide == j) & (tall == i), entry, upper)
    upper_ref[...] = upper[:size, :size]


def body(operator, adjacency, counts, rhs, start, shifts):
    elems, width, columns = operator.shape
    steps = shifts.shape[0]
    devices = lax.axis_size(AXES)
    slabs = lax.axis_size("slab")
    groups = lax.axis_size("group")
    packed = elems * width // LANES
    size = steps + 1
    vmem = pl.BlockSpec(memory_space=pltpu.VMEM)
    smem = pl.BlockSpec(memory_space=pltpu.SMEM)
    hbm = pl.BlockSpec(memory_space=pl.ANY)
    mebi = 1024 * 1024
    f32 = jnp.float32

    x = start.reshape(packed, LANES)
    b = rhs.reshape(packed, LANES)
    sources = (operator, adjacency.T, counts, x, b)
    made = (RIM * ROWS + 2 * packed, BODY * ROWS, INNER * ROWS + 2 * packed)
    rim, middle, inner = pl.pallas_call(
        band_kernel,
        out_shape=tuple(pltpu.VMEM((rows, LANES), f32) for rows in made),
        in_specs=[hbm] * 5,
        out_specs=(vmem, vmem, vmem),
        scratch_shapes=[
            pltpu.VMEM(operator.shape, f32),
            pltpu.SMEM(adjacency.T.shape, jnp.int32),
            pltpu.SMEM(counts.shape, jnp.int32),
            pltpu.SemaphoreType.DMA((elems // CHUNK,)),
            pltpu.SemaphoreType.DMA((6,)),
        ],
        compiler_params=pltpu.CompilerParams(vmem_limit_bytes=16 * mebi),
        name="bands",
    )(*(pltpu.with_memory_space_constraint(source, pltpu.HBM) for source in sources))
    far_rim = between_chips(rim)
    far_body = between_chips(middle)
    far_inner = within_chip(inner)
    first, last = pl.pallas_call(
        early_kernel,
        out_shape=(
            jax.ShapeDtypeStruct((16, LANES), f32),
            jax.ShapeDtypeStruct((packed, LANES), f32),
        ),
        in_specs=[vmem] * 5 + [smem],
        out_specs=(vmem, vmem),
        scratch_shapes=[pltpu.VMEM((4 * LEVEL, LANES), f32)],
        compiler_params=pltpu.CompilerParams(vmem_limit_bytes=16 * mebi),
        cost_estimate=pl.CostEstimate(flops=20 * 10**9, bytes_accessed=0, transcendentals=0),
        name="early",
    )(rim, middle, inner, far_rim, far_inner, shifts)
    basis, gram = pl.pallas_call(
        functools.partial(late_kernel, size),
        out_shape=(
            jax.ShapeDtypeStruct((8 * size, LANES), f32),
            jax.ShapeDtypeStruct((slabs, LANES), f32),
        ),
        in_specs=[vmem] * 9 + [smem],
        out_specs=(vmem, vmem),
        scratch_shapes=[pltpu.VMEM(((size - 1) * LEVEL, LANES), f32)],
        compiler_params=pltpu.CompilerParams(vmem_limit_bytes=16 * mebi),
        name="late",
    )(
        within_chip(last), between_chips(last), rim, middle, inner, far_rim, far_inner, far_body,
        first, shifts,
    )
    parts = lax.all_to_all(gram, "slab", 0, 0, tiled=True)
    parts = pl.pallas_call(
        partial_kernel,
        out_shape=jax.ShapeDtypeStruct((groups, LANES), f32),
        in_specs=[vmem],
        out_specs=vmem,
        compiler_params=pltpu.CompilerParams(vmem_limit_bytes=4 * mebi),
        name="partial",
    )(parts)
    parts = lax.all_to_all(parts, "group", 0, 0, tiled=True)
    sol, res, upper = pl.pallas_call(
        functools.partial(finish_kernel, devices * elems * width, steps),
        out_shape=(
            jax.ShapeDtypeStruct((packed, LANES), f32),
            jax.ShapeDtypeStruct((packed, LANES), f32),
            jax.ShapeDtypeStruct((steps + 1, steps + 1), f32),
        ),
        in_specs=[vmem, vmem, vmem, smem],
        out_specs=(vmem, vmem, vmem),
        compiler_params=pltpu.CompilerParams(vmem_limit_bytes=4 * mebi),
        name="finish",
    )(parts, basis, x, shifts)
    return (sol.reshape(-1), res.reshape(-1), upper)


def solution(mesh):
    split = P(AXES)
    return jax.shard_map(
        body,
        mesh=mesh,
        in_specs=(P(AXES, None, None), P(AXES, None), split, split, split, P()),
        out_specs=(split, split, P()),
        check_vma=False,
    )
```

```python
import functools

import jax
import jax.numpy as jnp
from jax import lax
from jax.experimental import pallas as pl
from jax.experimental.pallas import tpu as pltpu
from jax.sharding import PartitionSpec as P

AXES = ("group", "slab")
WIDTH = 64
LANES = 128
REACH = 2
BANDS = 2 * REACH + 1
HALF = WIDTH // 2
ROWS = BANDS * HALF
CHUNK = 4
GROUP = 8
MOST = 14
PAD = 6
LEVEL = 56


def between_chips(array):
    size = lax.axis_size(AXES)
    pairs = [(i, i + 1 if i % 2 else i - 1) for i in range(1, size - 1)]
    return lax.ppermute(array, AXES, pairs)


def within_chip(array):
    size = lax.axis_size(AXES)
    return lax.ppermute(array, AXES, [(i, i + 1 - 2 * (i % 2)) for i in range(size)])


def across(array):
    size = lax.axis_size(AXES)
    pairs = [(i, i + 4 * (i % 2) - 2) for i in range(size)]
    return lax.ppermute(array, AXES, [(i, j) for i, j in pairs if 0 <= j < size])


def lane_ids(rows):
    return lax.broadcasted_iota(jnp.int32, (rows, LANES), 1)


def band_kernel(
    op_ref, adjacency_ref, valid_ref, start_ref, rhs_ref, most_ref, outer_ref, inner_ref,
    held, adj_ref, counts_ref, in_sems, other_sems,
):
    elems, _, columns = op_ref.shape
    faces = columns // WIDTH - 1
    chunks = elems // CHUNK
    device = lax.axis_index(AXES)
    base = device * elems
    second = device % 2
    left = lane_ids(HALF) < WIDTH

    def origin(chunk):
        return jnp.where(second == 1, elems - CHUNK * (chunk + 1), CHUNK * chunk)

    def arriving(chunk):
        part = pl.ds(origin(chunk), CHUNK)
        return pltpu.make_async_copy(op_ref.at[part], held.at[part], in_sems.at[chunk])

    for chunk in range(chunks):
        arriving(chunk).start()
    scalars = [
        pltpu.make_async_copy(adjacency_ref, adj_ref, other_sems.at[0]),
        pltpu.make_async_copy(valid_ref, counts_ref, other_sems.at[1]),
    ]
    extras = []
    for number, source in enumerate((start_ref, rhs_ref)):
        for place, (target, size) in enumerate(((most_ref, MOST), (inner_ref, GROUP))):
            rows = pl.ds(size * ROWS + 8 * number, 8)
            sem = other_sems.at[2 + 2 * number + place]
            extras.append(pltpu.make_async_copy(source, target.at[rows, :], sem))
    for copy in scalars + extras:
        copy.start()
    for copy in scalars:
        copy.wait()

    def one(e, targets):
        blocks = []
        for tile in range(columns // LANES):
            lanes = pl.ds(tile * LANES, LANES)
            top = held[e, pl.ds(0, HALF), lanes]
            low = held[e, pl.ds(HALF, HALF), lanes]
            blocks.append(jnp.where(left, top, pltpu.roll(low, WIDTH, 1)))
            blocks.append(jnp.where(left, pltpu.roll(top, WIDTH, 1), low))
        if columns % LANES:
            lanes = pl.ds(columns - WIDTH, WIDTH)
            top = held[e, pl.ds(0, HALF), lanes]
            low = held[e, pl.ds(HALF, HALF), lanes]
            blocks.append(jnp.concatenate([top, low], axis=1))
        count = counts_ref[e]
        place = []
        for face in range(faces):
            offset = adj_ref[face, e] - (base + e) + REACH
            place.append(jnp.where(face < count, offset, -1))
        for band in range(BANDS):
            total = blocks[0] if band == REACH else None
            if band != REACH:
                for face in range(faces):
                    weight = jnp.where(place[face] == band, jnp.float32(1), jnp.float32(0))
                    term = blocks[face + 1] * weight
                    total = term if total is None else total + term
            for target, at in targets:
                target[pl.ds(pl.multiple_of(at * ROWS + band * HALF, HALF), HALF), :] = total

    in_most = jnp.where(second == 1, elems - MOST, 0)
    in_outer = jnp.where(second == 1, GROUP, 0)
    in_inner = GROUP - in_outer

    def some(chunk, carry, target=outer_ref, start=in_outer):
        arriving(chunk).wait()
        for k in range(CHUNK):
            e = origin(chunk) + k
            one(e, [(most_ref, e - in_most), (target, e - start)])
        return carry

    lax.fori_loop(0, 2, some, 0)
    some(2, 0, target=inner_ref, start=in_inner)
    arriving(3).wait()
    for k in range(CHUNK):
        e = jnp.where(second == 1, CHUNK - 1 - k, elems - CHUNK + k)
        targets = [(inner_ref, e - in_inner)]
        if k < MOST - 3 * CHUNK:
            targets.append((most_ref, e - in_most))
        one(e, targets)
    for extra in extras:
        extra.wait()


def stacked_sums(terms, row):
    for span in (4, 2, 1):
        low = (row & span) == 0
        half = len(terms) // 2
        merged = []
        for a, b in zip(terms[:half], terms[half:]):
            kept = jnp.where(low, a, b)
            if span == 4:
                moved = pltpu.roll(jnp.where(low, b, a), 4, 0)
            else:
                moved = jnp.where(low, pltpu.roll(a, 8 - span, 0), pltpu.roll(b, span, 0))
            merged.append(kept + moved)
        terms = merged
    return terms[0]


def spread(ref, at, packed):
    left = lane_ids(8) < WIDTH
    turned = pltpu.roll(packed, WIDTH, 1)
    ref[pl.ds(at, 8, stride=2), :] = jnp.where(left, packed, turned)
    ref[pl.ds(at + 1, 8, stride=2), :] = jnp.where(left, turned, packed)


def times(find, place, vecs, at):
    row = lax.broadcasted_iota(jnp.int32, (8, LANES), 0)
    half = lane_ids(HALF)
    left = half < WIDTH
    spot = half % WIDTH - lax.broadcasted_iota(jnp.int32, (HALF, LANES), 0)
    near = [vecs[pl.ds(at + (k - REACH), 1), :] for k in range(GROUP + 2 * REACH)]
    terms = []
    for k in range(GROUP):
        ref, spare = find(place + k)
        total = None
        for band in range(BANDS):
            rows = pl.ds(spare * ROWS + band * HALF, HALF)
            term = ref[rows, :] * near[k + band]
            total = term if total is None else total + term
        top = jnp.sum(jnp.where(left, total, 0.0), axis=1, keepdims=True)
        low = jnp.sum(jnp.where(left, 0.0, total), axis=1, keepdims=True)
        placed = jnp.where(spot == 0, top, jnp.where(spot == HALF, low, 0.0))
        terms.append(jnp.sum(placed.reshape(HALF // 8, 8, LANES), axis=0))
    return stacked_sums(terms, row)


def row_of(place):
    return PAD + 2 * GROUP + place


def application(at, find, places, vecs, combine):
    made = []
    for place in places:
        fresh = times(find, place, vecs, at + row_of(place))
        made.append((row_of(place), combine(fresh, row_of(place))))
    for row, value in made:
        vecs[pl.ds(at + LEVEL + row, 8), :] = value


def by_core(run):
    second = lax.axis_index(AXES) % 2 == 1
    pl.when(second)(lambda: run(True))
    pl.when(jnp.logical_not(second))(lambda: run(False))


def finder(turned, outer, inner, far_inner, far_outer, far_most):
    arrays = ((far_most, -MOST, MOST), (outer, 0, 8), (inner, 8, 8), (far_inner, 16, 8), (far_outer, 24, 8))

    def find(place):
        out = 15 - place if turned else place
        for ref, first, size in arrays:
            if first <= out < first + size:
                return ref, first + size - 1 - out if turned else out - first
        raise ValueError(place)

    return find


def packed_rows(vecs, level):
    left = lane_ids(8) < WIDTH
    at = level * LEVEL + row_of(0)
    return jnp.where(left, vecs[pl.ds(at, 8, stride=2), :], vecs[pl.ds(at + 1, 8, stride=2), :])


def levels(plan, turned, find, vecs, shifts_ref):
    given = vecs.shape[0] - LEVEL

    def turn(index, carry, places):
        at = pl.multiple_of(index * LEVEL, 8)
        opening = index == 0
        source = pl.multiple_of(jnp.where(opening, given, at), 8)
        sign = jnp.where(opening, jnp.float32(-1), jnp.float32(1))
        scale = jnp.where(opening, jnp.float32(1), -shifts_ref[jnp.maximum(index - 1, 0)])
        application(
            at, find, places, vecs,
            lambda fresh, row: sign * fresh + scale * vecs[pl.ds(source + row, 8), :],
        )
        return carry

    for first, last, places in plan:
        if turned:
            places = [8 - place for place in places]
        if last - first == 1:
            turn(jnp.int32(first), 0, places)
        else:
            lax.fori_loop(first, last, functools.partial(turn, places=places), 0)


def two_rows(vecs, row, packed):
    packed = jnp.broadcast_to(packed, (8, LANES))
    turned = pltpu.roll(packed, WIDTH, 1)
    left = lane_ids(8) < WIDTH
    vecs[pl.ds(row, 1), :] = jnp.where(left, packed, turned)[:1]
    vecs[pl.ds(row + 1, 1), :] = jnp.where(left, turned, packed)[:1]


def early_kernel(plan, outer, inner, far_inner, far_outer, shifts_ref, vecs, opening_ref):
    empty = jnp.zeros((8, LANES), jnp.float32)
    for at in range(0, vecs.shape[0], 8):
        vecs[pl.ds(at, 8), :] = empty
    given = vecs.shape[0] - LEVEL

    def run(turned):
        find = finder(turned, outer, inner, far_inner, far_outer, None)
        for ref, place in ((inner, 0), (far_inner, -16 if turned else 16)):
            spread(vecs, row_of(place), ref[pl.ds(GROUP * ROWS, 8), :])
            spread(vecs, given + row_of(place), ref[pl.ds(GROUP * ROWS + 8, 8), :])
        levels(plan, turned, find, vecs, shifts_ref)

    by_core(run)
    opening_ref[...] = packed_rows(vecs, 1)


def late_kernel(
    plan, size, far_x, outer, inner, far_inner, far_outer, far_opening, far_most, early_ref, shifts_ref,
    basis_ref, gram_ref, vecs,
):
    for at in range(0, vecs.shape[0], 8):
        vecs[pl.ds(at, 8), :] = early_ref[pl.ds(at, 8), :]
    given = vecs.shape[0] - LEVEL

    def run(turned):
        find = finder(turned, outer, inner, far_inner, far_outer, far_most)
        place = 16 if turned else -16
        spread(vecs, row_of(place), far_most[pl.ds(MOST * ROWS, 8), :])
        spread(vecs, given + row_of(place), far_most[pl.ds(MOST * ROWS + 8, 8), :])
        if turned:
            two_rows(vecs, row_of(-18), far_x[pl.ds(7, 1), :])
            two_rows(vecs, LEVEL + row_of(30), far_opening[pl.ds(7, 1), :])
        else:
            two_rows(vecs, row_of(32), far_x[pl.ds(0, 1), :])
            two_rows(vecs, LEVEL + row_of(-16), far_opening[pl.ds(0, 1), :])
        levels(plan, turned, find, vecs, shifts_ref)

    by_core(run)
    rows = [packed_rows(vecs, k + 1) for k in range(size)]
    for k in range(size):
        basis_ref[pl.ds(8 * k, 8), :] = rows[k]
    lane = lane_ids(8)
    total = jnp.zeros((8, LANES), jnp.float32)
    number = 0
    for i in range(size):
        for j in range(i, size):
            entry = jnp.sum(rows[i] * rows[j], axis=1, keepdims=True)
            total = jnp.where(lane == number, entry, total)
            number += 1
    gram = jnp.sum(total, axis=0, keepdims=True)
    gram_ref[...] = jnp.broadcast_to(gram, gram_ref.shape)


def plans(size):
    early, late = [], []
    for k in range(size):
        low, high = REACH * (k + 1), 30 - REACH * k
        first = [p for p in (2, 10, 18, 24) if p + 8 > low and p < high and low < high]
        if 24 in first and 26 >= high:
            first.remove(24)
        last = [p for p in (-14, -6, 2, 10) if p < low and p + 8 > max(-14, low - 18)]
        last += [p for p in (16, 24) if p <= high < p + 8]
        for plan, places in ((early, first), (late, last)):
            if plan and plan[-1][2] == places:
                plan[-1] = (plan[-1][0], k + 1, places)
            elif places:
                plan.append((k, k + 1, places))
    return early, late


def partial_kernel(parts_ref, out_ref):
    total = jnp.sum(parts_ref[...], axis=0, keepdims=True)
    out_ref[...] = jnp.broadcast_to(total, out_ref.shape)


def inverse_root(value):
    guess = lax.rsqrt(value)
    return guess * (1.5 - 0.5 * value * guess * guess)


def finish_kernel(count, steps, parts_ref, basis_ref, start_ref, shifts_ref, sol_ref, res_ref, upper_ref):
    size = steps + 1
    lane = lane_ids(8)
    summed = jnp.broadcast_to(jnp.sum(parts_ref[...], axis=0, keepdims=True), (8, LANES))
    gram = {}
    number = 0
    for i in range(size):
        for j in range(i, size):
            entry = jnp.sum(jnp.where(lane == number, summed, 0.0), axis=1, keepdims=True)
            gram[i, j] = jnp.broadcast_to(entry, (8, LANES))
            number += 1
    factor = {}
    for k in range(size):
        turn = inverse_root(gram[k, k])
        for j in range(k, size):
            factor[k, j] = gram[k, j] * turn
        for i in range(k + 1, size):
            for j in range(i, size):
                gram[i, j] = gram[i, j] - factor[k, i] * factor[k, j]
    hess = {}
    for k in range(steps):
        for i in range(k + 1):
            hess[i, k] = factor[i, k] * shifts_ref[k] + factor[i, k + 1]
        hess[k + 1, k] = factor[k + 1, k + 1]
    target = [factor[0, 0]] + [jnp.zeros((8, LANES), jnp.float32)] * steps
    inverse = []
    for k in range(steps):
        a, b = hess[k, k], hess[k + 1, k]
        scale = inverse_root(a * a + b * b)
        cos, sin = a * scale, b * scale
        inverse.append(scale)
        for j in range(k + 1, steps):
            up, down = hess[k, j], hess[k + 1, j]
            hess[k, j] = cos * up + sin * down
            hess[k + 1, j] = cos * down - sin * up
        target[k], target[k + 1] = cos * target[k], -(sin * target[k])
    coeffs = [None] * steps
    for k in range(steps - 1, -1, -1):
        value = target[k]
        for j in range(k + 1, steps):
            value = value - hess[k, j] * coeffs[j]
        coeffs[k] = value * inverse[k]
    rows = [basis_ref[pl.ds(8 * k, 8), :] for k in range(size)]
    sol, res = 0.0, 0.0
    for k in range(steps):
        sol = sol + coeffs[k] * rows[k]
        res = res + coeffs[k] * (rows[k + 1] + shifts_ref[k] * rows[k])
    sol_ref[...] = start_ref[...] + sol
    res_ref[...] = rows[0] - res
    wide = lane_ids(16)
    tall = lax.broadcasted_iota(jnp.int32, (16, LANES), 0)
    scale = 1.0 / (count ** 0.5)
    upper = jnp.zeros((16, LANES), jnp.float32)
    for i in range(size):
        for j in range(i, size):
            entry = jnp.concatenate([factor[i, j]] * 2, axis=0) * scale
            upper = jnp.where((wide == j) & (tall == i), entry, upper)
    upper_ref[...] = upper[:size, :size]


def body(operator, adjacency, counts, rhs, start, shifts):
    elems, width, columns = operator.shape
    steps = shifts.shape[0]
    devices = lax.axis_size(AXES)
    slabs = lax.axis_size("slab")
    groups = lax.axis_size("group")
    packed = elems * width // LANES
    size = steps + 1
    vmem = pl.BlockSpec(memory_space=pltpu.VMEM)
    smem = pl.BlockSpec(memory_space=pltpu.SMEM)
    hbm = pl.BlockSpec(memory_space=pl.ANY)
    mebi = 1024 * 1024
    f32 = jnp.float32

    x = start.reshape(packed, LANES)
    b = rhs.reshape(packed, LANES)
    sources = (operator, adjacency.T, counts, x, b)
    early, late = plans(size)
    rows = (size + 2) * LEVEL
    made = (MOST * ROWS + 2 * packed, GROUP * ROWS, GROUP * ROWS + 2 * packed)
    most, outer, inner = pl.pallas_call(
        band_kernel,
        out_shape=tuple(pltpu.VMEM((count, LANES), f32) for count in made),
        in_specs=[hbm] * 5,
        out_specs=(vmem, vmem, vmem),
        scratch_shapes=[
            pltpu.VMEM(operator.shape, f32),
            pltpu.SMEM(adjacency.T.shape, jnp.int32),
            pltpu.SMEM(counts.shape, jnp.int32),
            pltpu.SemaphoreType.DMA((elems // CHUNK,)),
            pltpu.SemaphoreType.DMA((6,)),
        ],
        compiler_params=pltpu.CompilerParams(vmem_limit_bytes=16 * mebi),
        name="bands",
    )(*(pltpu.with_memory_space_constraint(source, pltpu.HBM) for source in sources))
    far_most = between_chips(most)
    chip = (outer, inner, within_chip(inner), within_chip(outer))
    held, opening = pl.pallas_call(
        functools.partial(early_kernel, early),
        out_shape=(
            jax.ShapeDtypeStruct((rows, LANES), f32),
            jax.ShapeDtypeStruct((packed, LANES), f32),
        ),
        in_specs=[vmem] * 4 + [smem],
        out_specs=(vmem, vmem),
        compiler_params=pltpu.CompilerParams(vmem_limit_bytes=16 * mebi),
        name="early",
    )(*chip, shifts)
    basis, gram = pl.pallas_call(
        functools.partial(late_kernel, late, size),
        out_shape=(
            jax.ShapeDtypeStruct((8 * size, LANES), f32),
            jax.ShapeDtypeStruct((slabs, LANES), f32),
        ),
        in_specs=[vmem] * 8 + [smem],
        out_specs=(vmem, vmem),
        scratch_shapes=[pltpu.VMEM((rows, LANES), f32)],
        compiler_params=pltpu.CompilerParams(vmem_limit_bytes=16 * mebi),
        name="late",
    )(across(x), *chip, between_chips(opening), far_most, held, shifts)
    parts = lax.all_to_all(gram, "slab", 0, 0, tiled=True)
    parts = pl.pallas_call(
        partial_kernel,
        out_shape=jax.ShapeDtypeStruct((groups, LANES), f32),
        in_specs=[vmem],
        out_specs=vmem,
        compiler_params=pltpu.CompilerParams(vmem_limit_bytes=4 * mebi),
        name="partial",
    )(parts)
    parts = lax.all_to_all(parts, "group", 0, 0, tiled=True)
    sol, res, upper = pl.pallas_call(
        functools.partial(finish_kernel, devices * elems * width, steps),
        out_shape=(
            jax.ShapeDtypeStruct((packed, LANES), f32),
            jax.ShapeDtypeStruct((packed, LANES), f32),
            jax.ShapeDtypeStruct((steps + 1, steps + 1), f32),
        ),
        in_specs=[vmem, vmem, vmem, smem],
        out_specs=(vmem, vmem, vmem),
        compiler_params=pltpu.CompilerParams(vmem_limit_bytes=4 * mebi),
        name="finish",
    )(parts, basis, x, shifts)
    return (sol.reshape(-1), res.reshape(-1), upper)


def solution(mesh):
    split = P(AXES)
    return jax.shard_map(
        body,
        mesh=mesh,
        in_specs=(P(AXES, None, None), P(AXES, None), split, split, split, P()),
        out_specs=(split, split, P()),
        check_vma=False,
    )
```

```python
import functools

import jax
import jax.numpy as jnp
from jax import lax
from jax.experimental import pallas as pl
from jax.experimental.pallas import tpu as pltpu
from jax.sharding import PartitionSpec as P

AXES = ("group", "slab")
WIDTH = 64
LANES = 128
REACH = 2
BANDS = 2 * REACH + 1
HALF = WIDTH // 2
ROWS = BANDS * HALF
CHUNK = 4
GROUP = 8
MOST = 14
PAD = 6
LEVEL = 56


def between_chips(array):
    size = lax.axis_size(AXES)
    pairs = [(i, i + 1 if i % 2 else i - 1) for i in range(1, size - 1)]
    return lax.ppermute(array, AXES, pairs)


def within_chip(array):
    size = lax.axis_size(AXES)
    return lax.ppermute(array, AXES, [(i, i + 1 - 2 * (i % 2)) for i in range(size)])


def across(array):
    size = lax.axis_size(AXES)
    pairs = [(i, i + 4 * (i % 2) - 2) for i in range(size)]
    return lax.ppermute(array, AXES, [(i, j) for i, j in pairs if 0 <= j < size])


def lane_ids(rows):
    return lax.broadcasted_iota(jnp.int32, (rows, LANES), 1)


def band_kernel(
    op_ref, adjacency_ref, valid_ref, start_ref, rhs_ref, most_ref, outer_ref, inner_ref,
    held, adj_ref, counts_ref, in_sems, other_sems,
):
    elems, _, columns = op_ref.shape
    faces = columns // WIDTH - 1
    chunks = elems // CHUNK
    device = lax.axis_index(AXES)
    base = device * elems
    second = device % 2
    left = lane_ids(HALF) < WIDTH

    def origin(chunk):
        return jnp.where(second == 1, elems - CHUNK * (chunk + 1), CHUNK * chunk)

    def arriving(chunk):
        part = pl.ds(origin(chunk), CHUNK)
        return pltpu.make_async_copy(op_ref.at[part], held.at[part], in_sems.at[chunk])

    for chunk in range(chunks):
        arriving(chunk).start()
    scalars = [
        pltpu.make_async_copy(adjacency_ref, adj_ref, other_sems.at[0]),
        pltpu.make_async_copy(valid_ref, counts_ref, other_sems.at[1]),
    ]
    extras = []
    for number, source in enumerate((start_ref, rhs_ref)):
        for place, (target, size) in enumerate(((most_ref, MOST), (inner_ref, GROUP))):
            rows = pl.ds(size * ROWS + 8 * number, 8)
            sem = other_sems.at[2 + 2 * number + place]
            extras.append(pltpu.make_async_copy(source, target.at[rows, :], sem))
    for copy in scalars + extras:
        copy.start()
    for copy in scalars:
        copy.wait()

    def one(e, targets):
        blocks = []
        for tile in range(columns // LANES):
            lanes = pl.ds(tile * LANES, LANES)
            top = held[e, pl.ds(0, HALF), lanes]
            low = held[e, pl.ds(HALF, HALF), lanes]
            blocks.append(jnp.where(left, top, pltpu.roll(low, WIDTH, 1)))
            blocks.append(jnp.where(left, pltpu.roll(top, WIDTH, 1), low))
        if columns % LANES:
            lanes = pl.ds(columns - WIDTH, WIDTH)
            top = held[e, pl.ds(0, HALF), lanes]
            low = held[e, pl.ds(HALF, HALF), lanes]
            blocks.append(jnp.concatenate([top, low], axis=1))
        count = counts_ref[e]
        place = []
        for face in range(faces):
            offset = adj_ref[face, e] - (base + e) + REACH
            place.append(jnp.where(face < count, offset, -1))
        for band in range(BANDS):
            total = blocks[0] if band == REACH else None
            if band != REACH:
                for face in range(faces):
                    weight = jnp.where(place[face] == band, jnp.float32(1), jnp.float32(0))
                    term = blocks[face + 1] * weight
                    total = term if total is None else total + term
            for target, at in targets:
                target[pl.ds(pl.multiple_of(at * ROWS + band * HALF, HALF), HALF), :] = total

    in_most = jnp.where(second == 1, elems - MOST, 0)
    in_outer = jnp.where(second == 1, GROUP, 0)
    in_inner = GROUP - in_outer

    def some(chunk, carry, target=outer_ref, start=in_outer):
        arriving(chunk).wait()
        for k in range(CHUNK):
            e = origin(chunk) + k
            one(e, [(most_ref, e - in_most), (target, e - start)])
        return carry

    lax.fori_loop(0, 2, some, 0)
    some(2, 0, target=inner_ref, start=in_inner)
    arriving(3).wait()
    for k in range(CHUNK):
        e = jnp.where(second == 1, CHUNK - 1 - k, elems - CHUNK + k)
        targets = [(inner_ref, e - in_inner)]
        if k < MOST - 3 * CHUNK:
            targets.append((most_ref, e - in_most))
        one(e, targets)
    for extra in extras:
        extra.wait()


def stacked_sums(terms, row):
    for span in (4, 2, 1):
        low = (row & span) == 0
        half = len(terms) // 2
        merged = []
        for a, b in zip(terms[:half], terms[half:]):
            kept = jnp.where(low, a, b)
            if span == 4:
                moved = pltpu.roll(jnp.where(low, b, a), 4, 0)
            else:
                moved = jnp.where(low, pltpu.roll(a, 8 - span, 0), pltpu.roll(b, span, 0))
            merged.append(kept + moved)
        terms = merged
    return terms[0]


def spread(ref, at, packed):
    left = lane_ids(8) < WIDTH
    turned = pltpu.roll(packed, WIDTH, 1)
    ref[pl.ds(at, 8, stride=2), :] = jnp.where(left, packed, turned)
    ref[pl.ds(at + 1, 8, stride=2), :] = jnp.where(left, turned, packed)


def times(find, place, vecs, at):
    row = lax.broadcasted_iota(jnp.int32, (8, LANES), 0)
    half = lane_ids(HALF)
    left = half < WIDTH
    spot = half % WIDTH - lax.broadcasted_iota(jnp.int32, (HALF, LANES), 0)
    near = [vecs[pl.ds(at + (k - REACH), 1), :] for k in range(GROUP + 2 * REACH)]
    terms = []
    for k in range(GROUP):
        ref, spare = find(place + k)
        total = None
        for band in range(BANDS):
            rows = pl.ds(spare * ROWS + band * HALF, HALF)
            term = ref[rows, :] * near[k + band]
            total = term if total is None else total + term
        top = jnp.sum(jnp.where(left, total, 0.0), axis=1, keepdims=True)
        low = jnp.sum(jnp.where(left, 0.0, total), axis=1, keepdims=True)
        placed = jnp.where(spot == 0, top, jnp.where(spot == HALF, low, 0.0))
        terms.append(jnp.sum(placed.reshape(HALF // 8, 8, LANES), axis=0))
    return stacked_sums(terms, row)


def row_of(place):
    return PAD + 2 * GROUP + place


def application(at, find, places, vecs, combine):
    made = []
    for place in places:
        fresh = times(find, place, vecs, at + row_of(place))
        made.append((row_of(place), combine(fresh, row_of(place))))
    for row, value in made:
        vecs[pl.ds(at + LEVEL + row, 8), :] = value


def by_core(run):
    second = lax.axis_index(AXES) % 2 == 1
    pl.when(second)(lambda: run(True))
    pl.when(jnp.logical_not(second))(lambda: run(False))


def finder(turned, outer, inner, far_inner, far_outer, far_most):
    arrays = ((far_most, -MOST, MOST), (outer, 0, 8), (inner, 8, 8), (far_inner, 16, 8), (far_outer, 24, 8))

    def find(place):
        out = 15 - place if turned else place
        for ref, first, size in arrays:
            if first <= out < first + size:
                return ref, first + size - 1 - out if turned else out - first
        raise ValueError(place)

    return find


def packed_rows(vecs, level):
    left = lane_ids(8) < WIDTH
    at = level * LEVEL + row_of(0)
    return jnp.where(left, vecs[pl.ds(at, 8, stride=2), :], vecs[pl.ds(at + 1, 8, stride=2), :])


def levels(plan, turned, find, vecs, shifts_ref):
    given = vecs.shape[0] - LEVEL

    def turn(index, carry, places):
        at = pl.multiple_of(index * LEVEL, 8)
        opening = index == 0
        source = pl.multiple_of(jnp.where(opening, given, at), 8)
        sign = jnp.where(opening, jnp.float32(-1), jnp.float32(1))
        scale = jnp.where(opening, jnp.float32(1), -shifts_ref[jnp.maximum(index - 1, 0)])
        application(
            at, find, places, vecs,
            lambda fresh, row: sign * fresh + scale * vecs[pl.ds(source + row, 8), :],
        )
        return carry

    for first, last, places in plan:
        if turned:
            places = [8 - place for place in places]
        if last - first == 1:
            turn(jnp.int32(first), 0, places)
        else:
            lax.fori_loop(first, last, functools.partial(turn, places=places), 0)


def two_rows(vecs, row, packed):
    packed = jnp.broadcast_to(packed, (8, LANES))
    turned = pltpu.roll(packed, WIDTH, 1)
    left = lane_ids(8) < WIDTH
    vecs[pl.ds(row, 1), :] = jnp.where(left, packed, turned)[:1]
    vecs[pl.ds(row + 1, 1), :] = jnp.where(left, turned, packed)[:1]


def start_levels(vecs, turned, inner, far_inner):
    empty = jnp.zeros((8, LANES), jnp.float32)
    for at in range(0, vecs.shape[0], 8):
        vecs[pl.ds(at, 8), :] = empty
    given = vecs.shape[0] - LEVEL
    for ref, place in ((inner, 0), (far_inner, -16 if turned else 16)):
        spread(vecs, row_of(place), ref[pl.ds(GROUP * ROWS, 8), :])
        spread(vecs, given + row_of(place), ref[pl.ds(GROUP * ROWS + 8, 8), :])


def opening_kernel(inner, far_inner, shifts_ref, opening_ref, start_ref, vecs):
    def run(turned):
        start_levels(vecs, turned, inner, far_inner)
        find = finder(turned, None, inner, far_inner, None, None)
        levels([(0, 1, [10])], turned, find, vecs, shifts_ref)

    by_core(run)
    opening_ref[...] = packed_rows(vecs, 1)
    start_ref[...] = inner[pl.ds(GROUP * ROWS, 8), :]


def early_kernel(plan, outer, inner, far_inner, far_outer, shifts_ref, vecs):
    def run(turned):
        start_levels(vecs, turned, inner, far_inner)
        find = finder(turned, outer, inner, far_inner, far_outer, None)
        levels(plan, turned, find, vecs, shifts_ref)

    by_core(run)


def late_kernel(
    plan, size, far_opening, outer, inner, far_inner, far_outer, far_x, far_most, early_ref, shifts_ref,
    basis_ref, gram_ref, vecs,
):
    for at in range(0, vecs.shape[0], 8):
        vecs[pl.ds(at, 8), :] = early_ref[pl.ds(at, 8), :]
    given = vecs.shape[0] - LEVEL

    def run(turned):
        find = finder(turned, outer, inner, far_inner, far_outer, far_most)
        place = 16 if turned else -16
        spread(vecs, row_of(place), far_most[pl.ds(MOST * ROWS, 8), :])
        spread(vecs, given + row_of(place), far_most[pl.ds(MOST * ROWS + 8, 8), :])
        if turned:
            two_rows(vecs, row_of(-18), far_x[pl.ds(7, 1), :])
            two_rows(vecs, LEVEL + row_of(30), far_opening[pl.ds(7, 1), :])
        else:
            two_rows(vecs, row_of(32), far_x[pl.ds(0, 1), :])
            two_rows(vecs, LEVEL + row_of(-16), far_opening[pl.ds(0, 1), :])
        levels(plan, turned, find, vecs, shifts_ref)

    by_core(run)
    rows = [packed_rows(vecs, k + 1) for k in range(size)]
    for k in range(size):
        basis_ref[pl.ds(8 * k, 8), :] = rows[k]
    lane = lane_ids(8)
    total = jnp.zeros((8, LANES), jnp.float32)
    number = 0
    for i in range(size):
        for j in range(i, size):
            entry = jnp.sum(rows[i] * rows[j], axis=1, keepdims=True)
            total = jnp.where(lane == number, entry, total)
            number += 1
    gram = jnp.sum(total, axis=0, keepdims=True)
    gram_ref[...] = jnp.broadcast_to(gram, gram_ref.shape)


def plans(size):
    early, late = [], []
    for k in range(size):
        low, high = REACH * (k + 1), 30 - REACH * k
        first = [p for p in (2, 10, 18, 24) if p + 8 > low and p < high and low < high]
        if 24 in first and 26 >= high:
            first.remove(24)
        last = [p for p in (-14, -6, 2, 10) if p < low and p + 8 > max(-14, low - 18)]
        last += [p for p in (16, 24) if p <= high < p + 8]
        for plan, places in ((early, first), (late, last)):
            if plan and plan[-1][2] == places:
                plan[-1] = (plan[-1][0], k + 1, places)
            elif places:
                plan.append((k, k + 1, places))
    return early, late


def partial_kernel(parts_ref, out_ref):
    total = jnp.sum(parts_ref[...], axis=0, keepdims=True)
    out_ref[...] = jnp.broadcast_to(total, out_ref.shape)


def inverse_root(value):
    guess = lax.rsqrt(value)
    return guess * (1.5 - 0.5 * value * guess * guess)


def finish_kernel(count, steps, parts_ref, basis_ref, start_ref, shifts_ref, sol_ref, res_ref, upper_ref):
    size = steps + 1
    lane = lane_ids(8)
    summed = jnp.broadcast_to(jnp.sum(parts_ref[...], axis=0, keepdims=True), (8, LANES))
    gram = {}
    number = 0
    for i in range(size):
        for j in range(i, size):
            entry = jnp.sum(jnp.where(lane == number, summed, 0.0), axis=1, keepdims=True)
            gram[i, j] = jnp.broadcast_to(entry, (8, LANES))
            number += 1
    factor = {}
    for k in range(size):
        turn = inverse_root(gram[k, k])
        for j in range(k, size):
            factor[k, j] = gram[k, j] * turn
        for i in range(k + 1, size):
            for j in range(i, size):
                gram[i, j] = gram[i, j] - factor[k, i] * factor[k, j]
    hess = {}
    for k in range(steps):
        for i in range(k + 1):
            hess[i, k] = factor[i, k] * shifts_ref[k] + factor[i, k + 1]
        hess[k + 1, k] = factor[k + 1, k + 1]
    target = [factor[0, 0]] + [jnp.zeros((8, LANES), jnp.float32)] * steps
    inverse = []
    for k in range(steps):
        a, b = hess[k, k], hess[k + 1, k]
        scale = inverse_root(a * a + b * b)
        cos, sin = a * scale, b * scale
        inverse.append(scale)
        for j in range(k + 1, steps):
            up, down = hess[k, j], hess[k + 1, j]
            hess[k, j] = cos * up + sin * down
            hess[k + 1, j] = cos * down - sin * up
        target[k], target[k + 1] = cos * target[k], -(sin * target[k])
    coeffs = [None] * steps
    for k in range(steps - 1, -1, -1):
        value = target[k]
        for j in range(k + 1, steps):
            value = value - hess[k, j] * coeffs[j]
        coeffs[k] = value * inverse[k]
    rows = [basis_ref[pl.ds(8 * k, 8), :] for k in range(size)]
    sol, res = 0.0, 0.0
    for k in range(steps):
        sol = sol + coeffs[k] * rows[k]
        res = res + coeffs[k] * (rows[k + 1] + shifts_ref[k] * rows[k])
    sol_ref[...] = start_ref[...] + sol
    res_ref[...] = rows[0] - res
    wide = lane_ids(16)
    tall = lax.broadcasted_iota(jnp.int32, (16, LANES), 0)
    scale = 1.0 / (count ** 0.5)
    upper = jnp.zeros((16, LANES), jnp.float32)
    for i in range(size):
        for j in range(i, size):
            entry = jnp.concatenate([factor[i, j]] * 2, axis=0) * scale
            upper = jnp.where((wide == j) & (tall == i), entry, upper)
    upper_ref[...] = upper[:size, :size]


def body(operator, adjacency, counts, rhs, start, shifts):
    elems, width, columns = operator.shape
    steps = shifts.shape[0]
    devices = lax.axis_size(AXES)
    slabs = lax.axis_size("slab")
    groups = lax.axis_size("group")
    packed = elems * width // LANES
    size = steps + 1
    vmem = pl.BlockSpec(memory_space=pltpu.VMEM)
    smem = pl.BlockSpec(memory_space=pltpu.SMEM)
    hbm = pl.BlockSpec(memory_space=pl.ANY)
    mebi = 1024 * 1024
    f32 = jnp.float32

    x = start.reshape(packed, LANES)
    b = rhs.reshape(packed, LANES)
    sources = (operator, adjacency.T, counts, x, b)
    early, late = plans(size)
    rows = (size + 2) * LEVEL
    made = (MOST * ROWS + 2 * packed, GROUP * ROWS, GROUP * ROWS + 2 * packed)
    most, outer, inner = pl.pallas_call(
        band_kernel,
        out_shape=tuple(pltpu.VMEM((count, LANES), f32) for count in made),
        in_specs=[hbm] * 5,
        out_specs=(vmem, vmem, vmem),
        scratch_shapes=[
            pltpu.VMEM(operator.shape, f32),
            pltpu.SMEM(adjacency.T.shape, jnp.int32),
            pltpu.SMEM(counts.shape, jnp.int32),
            pltpu.SemaphoreType.DMA((elems // CHUNK,)),
            pltpu.SemaphoreType.DMA((6,)),
        ],
        compiler_params=pltpu.CompilerParams(vmem_limit_bytes=16 * mebi),
        name="bands",
    )(*(pltpu.with_memory_space_constraint(source, pltpu.HBM) for source in sources))
    far_most = between_chips(most)
    chip = (outer, inner, within_chip(inner), within_chip(outer))
    opening, sent = pl.pallas_call(
        opening_kernel,
        out_shape=(jax.ShapeDtypeStruct((packed, LANES), f32),) * 2,
        in_specs=[vmem] * 2 + [smem],
        out_specs=(vmem, vmem),
        scratch_shapes=[pltpu.VMEM((3 * LEVEL, LANES), f32)],
        compiler_params=pltpu.CompilerParams(vmem_limit_bytes=16 * mebi),
        name="opening",
    )(chip[1], chip[2], shifts)
    held = pl.pallas_call(
        functools.partial(early_kernel, early),
        out_shape=jax.ShapeDtypeStruct((rows, LANES), f32),
        in_specs=[vmem] * 4 + [smem],
        out_specs=vmem,
        compiler_params=pltpu.CompilerParams(vmem_limit_bytes=16 * mebi),
        name="early",
    )(*chip, shifts)
    basis, gram = pl.pallas_call(
        functools.partial(late_kernel, late, size),
        out_shape=(
            jax.ShapeDtypeStruct((8 * size, LANES), f32),
            jax.ShapeDtypeStruct((slabs, LANES), f32),
        ),
        in_specs=[vmem] * 8 + [smem],
        out_specs=(vmem, vmem),
        scratch_shapes=[pltpu.VMEM((rows, LANES), f32)],
        compiler_params=pltpu.CompilerParams(vmem_limit_bytes=16 * mebi),
        name="late",
    )(between_chips(opening), *chip, across(sent), far_most, held, shifts)
    parts = lax.all_to_all(gram, "slab", 0, 0, tiled=True)
    parts = pl.pallas_call(
        partial_kernel,
        out_shape=jax.ShapeDtypeStruct((groups, LANES), f32),
        in_specs=[vmem],
        out_specs=vmem,
        compiler_params=pltpu.CompilerParams(vmem_limit_bytes=4 * mebi),
        name="partial",
    )(parts)
    parts = lax.all_to_all(parts, "group", 0, 0, tiled=True)
    sol, res, upper = pl.pallas_call(
        functools.partial(finish_kernel, devices * elems * width, steps),
        out_shape=(
            jax.ShapeDtypeStruct((packed, LANES), f32),
            jax.ShapeDtypeStruct((packed, LANES), f32),
            jax.ShapeDtypeStruct((steps + 1, steps + 1), f32),
        ),
        in_specs=[vmem, vmem, vmem, smem],
        out_specs=(vmem, vmem, vmem),
        compiler_params=pltpu.CompilerParams(vmem_limit_bytes=4 * mebi),
        name="finish",
    )(parts, basis, x, shifts)
    return (sol.reshape(-1), res.reshape(-1), upper)


def solution(mesh):
    split = P(AXES)
    return jax.shard_map(
        body,
        mesh=mesh,
        in_specs=(P(AXES, None, None), P(AXES, None), split, split, split, P()),
        out_specs=(split, split, P()),
        check_vma=False,
    )
```
